32 devices in a mesh: groups: 2 (over x), blk: 16 (over z, y, core).
Axes of the slice: x: 2, y: 2, z: 4, core: 2. Of those that a mesh axis runs over, the one named last changes fastest.
Arguments:
- embeddings: bfloat16 [12288, 512], P(('groups', 'blk')), parts along dimension 0, may hold values from -24 to 24
- cluster_ids: int32 [12288], P(('groups', 'blk')), parts along dimension 0, may hold values from 0 to 63, as said below
- cluster_sizes: int32 [128], P('groups'), parts along dimension 0, may hold values from 12 to 960, as said below
Outputs:
- log_density: float32 [12288], P(('groups', 'blk')), parts along dimension 0
- centrality: float32 [12288], P(('groups', 'blk')), parts along dimension 0
The draws below stay inside these ranges and needn't reach their ends.
There are 2 independent parts, one for each index of `groups`. The reference program is written for one: setup_inputs(seed, part) draws one part's arguments, and reference() takes and returns one part's arrays. A program takes and returns all parts, laid end to end along the dimension named above; each array names one. Nothing has to cross between parts.
Inputs may be any that keep to these rules, and one draw needn't show every extreme that they name: cluster_sizes[c] is the number of rows whose cluster id is c; the sizes sum to 6144 and the largest is exactly 960. `cluster_ids`: rows are dealt to the devices of blk: with n the number of devices of blk and E_c the sum of cluster_sizes[c'] mod n over the clusters c' < c, device s holds cluster_sizes[c] // n rows of cluster c, plus one more exactly when (s - E_c) mod n < cluster_sizes[c] mod n. Within a device the rows stand in no particular order.
All inputs are finite; a program needn't handle non-finite values.
Results may differ from the reference program's by a relative error of at most 0.00065.
The reference program's roundings to bfloat16 on the way (of `unit`) count: a program that leaves them out, or rounds other values in their place, can miss the bound.
Values may be sent and summed in bfloat16 or wider, within the bound.
A program may use at most 64 MiB of HBM per device.

```python
import math
import jax
import jax.numpy as jnp
from jax import lax

D = 512
CLUSTERS = 64
ROWS = 6144
MOST = 960
N_BLK = 16


def window_layout(key):
    layout_key = jax.random.fold_in(key, 11)
    cut_key, perm_key, shuffle_key = jax.random.split(layout_key, 3)
    largest = ROWS * 5 // 32
    fewest = ROWS // 512
    leftover = ROWS - largest - (CLUSTERS - 1) * fewest
    stride = largest - fewest
    fixed_cuts = leftover // stride
    uneven_boundaries = CLUSTERS - 2 - fixed_cuts
    grid_cuts = jnp.arange(1, fixed_cuts + 1, dtype=jnp.int32) * stride
    random_cuts = jax.random.randint(cut_key, (uneven_boundaries,), 0, leftover + 1, dtype=jnp.int32)
    cuts = jnp.sort(jnp.concatenate([grid_cuts, random_cuts]))
    edges = jnp.concatenate([jnp.zeros((1,), jnp.int32), cuts, jnp.full((1,), leftover, jnp.int32)])
    pieces = edges[1:] - edges[:-1] + fewest
    sizes = jnp.concatenate([jnp.full((1,), largest, jnp.int32), pieces])
    sizes = sizes[jax.random.permutation(perm_key, CLUSTERS)]
    devices = N_BLK
    per_device = ROWS // devices
    base = sizes // devices
    extra = sizes % devices
    first = (jnp.cumsum(extra) - extra) % devices
    source_rows = jnp.arange(devices, dtype=jnp.int32)
    holds = base[None, :] + ((source_rows[:, None] - first[None, :]) % devices < extra[None, :]).astype(jnp.int32)
    running = jnp.cumsum(holds, axis=1)
    local = jnp.arange(per_device, dtype=jnp.int32)
    labels = jnp.sum((local[None, :, None] >= running[:, None, :]).astype(jnp.int32), axis=2)
    similarity_scores = jax.random.randint(shuffle_key, (devices, per_device), 0, per_device, dtype=jnp.int32) * per_device + local[None, :]
    shuffle = jnp.argsort(similarity_scores, axis=1)
    labels = jnp.take_along_axis(labels, shuffle, axis=1)
    return (sizes, labels.reshape(ROWS).astype(jnp.int32))


def draw_cluster_sizes(key, part):
    sizes, labels = window_layout(key)
    return sizes


def draw_cluster_ids(key, part):
    sizes, labels = window_layout(key)
    return labels


def draw_embeddings(key, part):
    sizes, labels = window_layout(key)
    center_key, amp_key, noise_key = jax.random.split(jax.random.fold_in(key, 23), 3)
    centers = jax.random.truncated_normal(center_key, -4.0, 4.0, (CLUSTERS, D), jnp.float32)
    amplitude = jnp.exp(jax.random.uniform(amp_key, (ROWS, 1), jnp.float32, math.log(0.2), math.log(3.0)))
    noise = jax.random.truncated_normal(noise_key, -4.0, 4.0, (ROWS, D), jnp.float32)
    values = amplitude * centers[labels] + noise
    return values.astype(jnp.bfloat16)


def setup_inputs(seed: int = 0, part: int = 0) -> dict:
    streams_of = jax.random.split(jax.random.key(seed), 4)
    own_keys = jax.random.split(jax.random.fold_in(streams_of[3], part), 4)
    return {
        "embeddings": draw_embeddings(jax.random.fold_in(jax.random.fold_in(streams_of[3], part), 71), part),
        "cluster_ids": draw_cluster_ids(jax.random.fold_in(jax.random.fold_in(streams_of[3], part), 71), part),
        "cluster_sizes": draw_cluster_sizes(jax.random.fold_in(jax.random.fold_in(streams_of[3], part), 71), part),
    }


SOFTMAX_TEMP = 0.1
EPSILON = 1e-06

def unit_rows(embeddings):
    values = embeddings.astype(jnp.float32)
    scale = lax.rsqrt(lax.optimization_barrier(jnp.mean(values * values, axis=1, keepdims=True)) + EPSILON)
    return (values * (scale * values.shape[1] ** (-0.5))).astype(jnp.bfloat16)

def block_terms(remaining_rows, left_labels, right_rows, right_labels):
    similarity_scores = jnp.dot(remaining_rows, right_rows.T, preferred_element_type=jnp.float32)
    same_cluster = left_labels[:, None] == right_labels[None, :]
    return lax.optimization_barrier(jnp.sum(jnp.where(same_cluster, jnp.exp(similarity_scores / SOFTMAX_TEMP), 0.0), axis=1))

def lookup(table, one_hot):
    return lax.optimization_barrier(jnp.sum(jnp.where(one_hot, table[None, :], 0), axis=1))

def reference(embeddings, cluster_ids, cluster_sizes):
    unit = unit_rows(embeddings)
    order = jnp.argsort(cluster_ids, stable=True).astype(jnp.int32)
    sorted_unit = unit[order]
    sorted_labels = cluster_ids[order]
    window = min(ROWS, 512 + 2 * MOST)

    def one_block(index):
        lower = (index * 512).astype(jnp.int32)
        begin = jnp.clip(lower - MOST, 0, ROWS - window).astype(jnp.int32)
        remaining_rows = lax.dynamic_slice_in_dim(sorted_unit, lower, 512)
        left_labels = lax.dynamic_slice_in_dim(sorted_labels, lower, 512)
        right_rows = lax.dynamic_slice_in_dim(sorted_unit, begin, window)
        right_labels = lax.dynamic_slice_in_dim(sorted_labels, begin, window)
        return block_terms(remaining_rows, left_labels, right_rows, right_labels)
    sorted_density = lax.map(one_block, jnp.arange(ROWS // 512, dtype=jnp.int32)).reshape(ROWS)
    density = jnp.zeros((ROWS,), jnp.float32).at[order].set(sorted_density)
    member = cluster_ids[:, None] == jnp.arange(CLUSTERS, dtype=jnp.int32)[None, :]
    sizes_row = lookup(cluster_sizes, member).astype(jnp.float32)
    log_density = jnp.log(density / sizes_row)
    unit_wide = unit.astype(jnp.float32)
    centroid = jnp.dot(member.astype(jnp.float32).T, unit_wide, precision=lax.Precision.HIGHEST)
    projected = jnp.dot(unit_wide, centroid.T, precision=lax.Precision.HIGHEST)
    centrality = lax.optimization_barrier(jnp.sum(jnp.where(member, projected, 0.0), axis=1)) / sizes_row
    return (log_density, centrality)
```

```python
import functools

import jax
import jax.numpy as jnp
from jax import lax
from jax.experimental import pallas as pl
from jax.experimental.pallas import tpu as pltpu
from jax.sharding import PartitionSpec as P

SOFTMAX_TEMP = 0.1
EPSILON = 1e-06
LANES = 128
MESH = pl.DeviceIdType.MESH
F32 = jnp.float32
BF16 = jnp.bfloat16
NT = (((1,), (1,)), ((), ()))


def iota(shape, dim):
    return lax.broadcasted_iota(jnp.int32, shape, dim)


def loop(count, body):
    if count <= 8:
        for step in range(count):
            body(step)
    else:
        lax.fori_loop(0, count, lambda step, carry: (body(step), carry)[1], 0)


def kernel(n, cap, limit, emb_ref, ids_ref, sizes_ref, dens_ref, cent_ref,
           packed, packed_lab, own, other, own_lab, other_lab, ret, ret_in, addr_ref,
           send, recv, send_lab, recv_lab, fsend, frecv, fsend_lab, frecv_lab, rsend, rrecv):
    bins = n // 2
    rows, width = emb_ref.shape
    clusters = sizes_ref.shape[1]
    me = lax.axis_index("blk")
    chip = lax.div(me, 2)
    core = lax.rem(me, 2)
    partner = 2 * chip + 1 - core

    def peer(step):
        return 2 * lax.rem(chip + step, bins) + core

    def back(step):
        return 2 * lax.rem(chip + bins - step, bins) + core

    barrier = pltpu.get_barrier_semaphore()
    pl.semaphore_signal(barrier, inc=1, device_id={"blk": partner}, device_id_type=MESH)
    loop(bins - 1, lambda s: pl.semaphore_signal(
        barrier, inc=1, device_id={"blk": peer(s + 1)}, device_id_type=MESH))

    values = emb_ref[...].astype(F32)
    scale = lax.rsqrt(jnp.mean(values * values, axis=1, keepdims=True) + EPSILON)
    unit = (values * (scale * width ** (-0.5))).astype(BF16)

    sizes_row = sizes_ref[...].astype(F32)
    above = iota((clusters, clusters), 0)
    along = iota((clusters, clusters), 1)
    ends = jnp.sum(jnp.where(along <= above, sizes_row, 0.0), axis=1, keepdims=True)
    sizes = jnp.sum(jnp.where(along == above, sizes_row, 0.0), axis=1, keepdims=True)
    starts = ends - sizes
    edge = jnp.zeros((1, 1), F32)
    bin_of = jnp.zeros((clusters, 1), F32)
    for _ in range(bins - 1):
        edge = jnp.max(jnp.where(ends <= edge + limit, ends, 0.0), axis=0, keepdims=True)
        bin_of += jnp.where(starts >= edge, 1.0, 0.0)

    ids = ids_ref[...]
    member = iota((clusters, rows), 0) == ids
    bin_row = jnp.sum(jnp.where(member, bin_of, 0.0), axis=0, keepdims=True)
    size_row = jnp.sum(jnp.where(member, sizes, 0.0), axis=0, keepdims=True)
    shown = max(bins, 8)
    in_bin = iota((shown, rows), 0).astype(F32) == bin_row
    before = jnp.where(iota((rows, rows), 0) < iota((rows, rows), 1), 1.0, 0.0).astype(BF16)
    rank = jnp.dot(jnp.where(in_bin, 1.0, 0.0).astype(BF16), before, preferred_element_type=F32)
    slot = jnp.sum(jnp.where(in_bin, rank, 0.0), axis=0, keepdims=True)
    address = (bin_row * LANES + slot).astype(jnp.int32)
    addr_ref[...] = jnp.broadcast_to(address, addr_ref.shape)
    label_rows = jnp.broadcast_to((ids + 1).astype(F32), (8, rows)).astype(BF16)

    def hot(step):
        place = lax.rem(chip + step, bins) * LANES
        return iota((LANES, rows), 0) + place == addr_ref[0:1, :]

    def data_copy(step):
        return pltpu.make_async_remote_copy(
            packed.at[step, pl.ds(0, cap)], own.at[step, pl.ds(0, cap)],
            send.at[step], recv.at[step], device_id={"blk": peer(step)}, device_id_type=MESH)

    def label_copy(step):
        return pltpu.make_async_remote_copy(
            packed_lab.at[step], own_lab.at[step], send_lab.at[step], recv_lab.at[step],
            device_id={"blk": peer(step)}, device_id_type=MESH)

    def forward_copy(step):
        return pltpu.make_async_remote_copy(
            own.at[step, pl.ds(0, cap)], other.at[step, pl.ds(0, cap)],
            fsend.at[step], frecv.at[step], device_id={"blk": partner}, device_id_type=MESH)

    def forward_label_copy(step):
        return pltpu.make_async_remote_copy(
            own_lab.at[step], other_lab.at[step], fsend_lab.at[step], frecv_lab.at[step],
            device_id={"blk": partner}, device_id_type=MESH)

    def return_copy(step):
        return pltpu.make_async_remote_copy(
            ret.at[step], ret_in.at[step], rsend.at[step], rrecv.at[step],
            device_id={"blk": back(step)}, device_id_type=MESH)

    def pack(step, rows_ref, lab_ref):
        one_hot = jnp.where(hot(step), 1.0, 0.0).astype(BF16)
        rows_ref[step] = jnp.dot(one_hot, unit, preferred_element_type=F32).astype(BF16)
        lab_ref[step] = lax.dot_general(label_rows, one_hot, NT, preferred_element_type=F32)

    pl.semaphore_wait(barrier, bins)

    def send_step(s):
        pack(s + 1, packed, packed_lab)
        data_copy(s + 1).start()
        label_copy(s + 1).start()

    loop(bins - 1, send_step)
    pack(0, own, own_lab)
    forward_copy(0).start()
    forward_label_copy(0).start()
    if cap < LANES:
        def clear(s):
            own[s + 1, cap:, :] = jnp.zeros((LANES - cap, width), BF16)
        loop(bins - 1, clear)

    def pass_on(s):
        data_copy(s + 1).wait_recv()
        forward_copy(s + 1).start()
        label_copy(s + 1).wait_recv()
        forward_label_copy(s + 1).start()

    loop(bins - 1, pass_on)

    def arrived(s):
        forward_copy(s).wait_recv()
        forward_label_copy(s).wait_recv()

    loop(bins, arrived)

    def scores(side, lab, pair, total):
        left = side[:, :cap, :].reshape(bins * cap, width)
        columns = lab[:, 0, :].T
        left_lab = jnp.concatenate([columns[:cap, s:s + 1] for s in range(bins)], axis=0)
        right = own[pl.ds(2 * pair, 2)].reshape(2 * LANES, width)
        right_lab = jnp.concatenate(
            [own_lab[2 * pair, 0:1, :], own_lab[2 * pair + 1, 0:1, :]], axis=1)
        cosine = lax.dot_general(left, right, NT, preferred_element_type=F32)
        same = left_lab == right_lab
        dens = jnp.sum(jnp.where(same, jnp.exp(cosine * (1.0 / SOFTMAX_TEMP)), 0.0),
                       axis=0, keepdims=True)
        cent = jnp.sum(jnp.where(same, cosine, 0.0), axis=0, keepdims=True)
        return total[0] + dens, total[1] + cent

    def work(pair):
        none = jnp.zeros((1, 2 * LANES), F32)
        total = scores(own, own_lab, pair, (none, none))
        dens, cent = scores(other, other_lab, pair, total)
        for half in range(2):
            part = slice(half * LANES, (half + 1) * LANES)
            ret[2 * pair + half] = jnp.concatenate(
                [dens[:, part], cent[:, part], jnp.zeros((6, LANES), F32)], axis=0)

    lax.fori_loop(0, bins // 2, lambda pair, carry: (work(pair), carry)[1], 0)
    loop(bins - 1, lambda s: return_copy(s + 1).start())
    ret_in[0] = ret[0]
    loop(bins - 1, lambda s: return_copy(s + 1).wait_recv())

    def gathered(step, total):
        answer = ret_in[step].T
        mine = hot(step)
        return (total[0] + jnp.where(mine, answer[:, 0:1], 0.0),
                total[1] + jnp.where(mine, answer[:, 1:2], 0.0))

    none = jnp.zeros((LANES, rows), F32)
    dens, cent = lax.fori_loop(0, bins, gathered, (none, none))
    dens_ref[...] = jnp.log(jnp.sum(dens, axis=0, keepdims=True) / size_row)
    cent_ref[...] = jnp.sum(cent, axis=0, keepdims=True) / size_row

    def finish(s):
        data_copy(s + 1).wait_send()
        label_copy(s + 1).wait_send()
        return_copy(s + 1).wait_send()

    loop(bins - 1, finish)

    def finish_forward(s):
        forward_copy(s).wait_send()
        forward_label_copy(s).wait_send()

    loop(bins, finish_forward)


def on_device(embeddings, cluster_ids, cluster_sizes):
    n = lax.axis_size("blk")
    rows, width = embeddings.shape
    bins = n // 2
    total = rows * n
    limit = max(2 * total // bins, total * 5 // 32)
    cap = -(-(-(-limit // n)) // 16) * 16
    vmem = pl.BlockSpec(memory_space=pltpu.VMEM)
    dma = pltpu.SemaphoreType.DMA((bins,))
    dens, cent = pl.pallas_call(
        functools.partial(kernel, n, cap, float(limit)),
        out_shape=[jax.ShapeDtypeStruct((1, rows), F32)] * 2,
        in_specs=[vmem] * 3,
        out_specs=[vmem] * 2,
        scratch_shapes=[
            pltpu.VMEM((bins, LANES, width), BF16),
            pltpu.VMEM((bins, 8, LANES), F32),
            pltpu.VMEM((bins, LANES, width), BF16),
            pltpu.VMEM((bins, LANES, width), BF16),
            pltpu.VMEM((bins, 8, LANES), F32),
            pltpu.VMEM((bins, 8, LANES), F32),
            pltpu.VMEM((bins, 8, LANES), F32),
            pltpu.VMEM((bins, 8, LANES), F32),
            pltpu.VMEM((8, rows), jnp.int32),
        ] + [dma] * 10,
        compiler_params=pltpu.CompilerParams(
            collective_id=0, has_side_effects=True, vmem_limit_bytes=48 * 1024 * 1024),
        cost_estimate=pl.CostEstimate(flops=4 * 10 ** 9, bytes_accessed=10 ** 6, transcendentals=0),
    )(embeddings, cluster_ids[None, :], cluster_sizes[None, :])
    return dens[0], cent[0]


def solution(mesh):
    in_specs = (P(("groups", "blk"), None), P(("groups", "blk")), P("groups"))
    out_specs = (P(("groups", "blk")), P(("groups", "blk")))
    return jax.shard_map(
        on_device, mesh=mesh, in_specs=in_specs, out_specs=out_specs, check_vma=False
    )
```

```python
import functools

import jax
import jax.numpy as jnp
from jax import lax
from jax.experimental import pallas as pl
from jax.experimental.pallas import tpu as pltpu
from jax.sharding import PartitionSpec as P

SOFTMAX_TEMP = 0.1
EPSILON = 1e-06
LANES = 128
MESH = pl.DeviceIdType.MESH
F32 = jnp.float32
BF16 = jnp.bfloat16
NT = (((1,), (1,)), ((), ()))


def iota(shape, dim):
    return lax.broadcasted_iota(jnp.int32, shape, dim)


def loop(count, body):
    if count <= 8:
        for step in range(count):
            body(step)
    else:
        lax.fori_loop(0, count, lambda step, carry: (body(step), carry)[1], 0)


def kernel(n, cap, limit, emb_hbm, ids_hbm, sizes_hbm, out_ref,
           emb, ids_ref, sizes_ref, packed, packed_lab, own, other, own_lab, other_lab, ret, ret_in, addr_ref,
           acc_dens, acc_cent, emb_sem, ids_sem, sizes_sem,
           send, recv, send_lab, recv_lab, fsend, frecv, fsend_lab, frecv_lab, rsend, rrecv):
    bins = n // 2
    rows, width = emb.shape
    clusters = sizes_ref.shape[0]
    me = lax.axis_index("blk")
    chip = lax.div(me, 2)
    core = lax.rem(me, 2)
    partner = 2 * chip + 1 - core

    def distance(place):
        if isinstance(place, int) and place == 0:
            return 0
        return bins // 2 + (2 * lax.rem(place, 2) - 1) * lax.div(place, 2)

    def peer(place):
        return 2 * lax.rem(chip + distance(place), bins) + core

    def back(place):
        return 2 * lax.rem(chip + bins - distance(place), bins) + core

    fetch = pltpu.make_async_copy(emb_hbm, emb, emb_sem)
    fetch_ids = pltpu.make_async_copy(ids_hbm, ids_ref, ids_sem)
    fetch_sizes = pltpu.make_async_copy(sizes_hbm, sizes_ref, sizes_sem)
    fetch_sizes.start()
    fetch_ids.start()
    fetch.start()
    barrier = pltpu.get_barrier_semaphore()
    pl.semaphore_signal(barrier, inc=1, device_id={"blk": partner}, device_id_type=MESH)
    loop(bins - 1, lambda s: pl.semaphore_signal(
        barrier, inc=1, device_id={"blk": peer(s + 1)}, device_id_type=MESH))

    fetch_sizes.wait()
    sizes_row = sizes_ref[...].reshape(1, clusters).astype(F32)
    above = iota((clusters, clusters), 0)
    along = iota((clusters, clusters), 1)
    ends = jnp.sum(jnp.where(along <= above, sizes_row, 0.0), axis=1, keepdims=True)
    sizes = jnp.sum(jnp.where(along == above, sizes_row, 0.0), axis=1, keepdims=True)
    starts = ends - sizes
    edge = jnp.zeros((1, 1), F32)
    bin_of = jnp.zeros((clusters, 1), F32)
    for _ in range(bins - 1):
        edge = jnp.max(jnp.where(ends <= edge + limit, ends, 0.0), axis=0, keepdims=True)
        bin_of += jnp.where(starts >= edge, 1.0, 0.0)

    fetch_ids.wait()
    ids = ids_ref[...].reshape(1, rows)
    member = iota((clusters, rows), 0) == ids
    bin_row = jnp.sum(jnp.where(member, bin_of, 0.0), axis=0, keepdims=True)
    size_row = jnp.sum(jnp.where(member, sizes, 0.0), axis=0, keepdims=True)
    shown = max(bins, 8)
    in_bin = iota((shown, rows), 0).astype(F32) == bin_row
    before = jnp.where(iota((rows, rows), 0) < iota((rows, rows), 1), 1.0, 0.0).astype(BF16)
    rank = jnp.dot(jnp.where(in_bin, 1.0, 0.0).astype(BF16), before, preferred_element_type=F32)
    slot = jnp.sum(jnp.where(in_bin, rank, 0.0), axis=0, keepdims=True)
    address = (bin_row * LANES + slot).astype(jnp.int32)
    addr_ref[...] = jnp.broadcast_to(address, addr_ref.shape)
    label_rows = jnp.broadcast_to((ids + 1).astype(F32), (8, rows)).astype(BF16)

    fetch.wait()
    values = emb[...].astype(F32)
    scale = lax.rsqrt(jnp.mean(values * values, axis=1, keepdims=True) + EPSILON)
    unit = (values * (scale * width ** (-0.5))).astype(BF16)

    def hot(place):
        first = lax.rem(chip + distance(place), bins) * LANES
        return iota((LANES, rows), 0) + first == addr_ref[0:1, :]

    def data_copy(place):
        return pltpu.make_async_remote_copy(
            packed.at[place, pl.ds(0, cap)], own.at[place, pl.ds(0, cap)],
            send.at[place], recv.at[place], device_id={"blk": peer(place)}, device_id_type=MESH)

    def label_copy(place):
        return pltpu.make_async_remote_copy(
            packed_lab.at[place], own_lab.at[place], send_lab.at[place], recv_lab.at[place],
            device_id={"blk": peer(place)}, device_id_type=MESH)

    def forward_copy(place):
        return pltpu.make_async_remote_copy(
            own.at[place, pl.ds(0, cap)], other.at[place, pl.ds(0, cap)],
            fsend.at[place], frecv.at[place], device_id={"blk": partner}, device_id_type=MESH)

    def forward_label_copy(place):
        return pltpu.make_async_remote_copy(
            own_lab.at[place], other_lab.at[place], fsend_lab.at[place], frecv_lab.at[place],
            device_id={"blk": partner}, device_id_type=MESH)

    def return_copy(place):
        return pltpu.make_async_remote_copy(
            ret.at[place], ret_in.at[place], rsend.at[place], rrecv.at[place],
            device_id={"blk": back(place)}, device_id_type=MESH)

    def pack(place, rows_ref, lab_ref):
        one_hot = jnp.where(hot(place), 1.0, 0.0).astype(BF16)
        rows_ref[place] = jnp.dot(one_hot, unit, preferred_element_type=F32).astype(BF16)
        lab_ref[place] = lax.dot_general(label_rows, one_hot, NT, preferred_element_type=F32)

    pl.semaphore_wait(barrier, bins)

    def send_step(s):
        pack(s + 1, packed, packed_lab)
        label_copy(s + 1).start()
        data_copy(s + 1).start()

    loop(bins - 1, send_step)
    pack(0, own, own_lab)
    forward_label_copy(0).start()
    forward_copy(0).start()
    if cap < LANES:
        def clear(s):
            own[s + 1, cap:, :] = jnp.zeros((LANES - cap, width), BF16)
        loop(bins - 1, clear)

    def clear_sums(pair):
        acc_dens[pair] = jnp.zeros((8, 2 * LANES), F32)
        acc_cent[pair] = jnp.zeros((8, 2 * LANES), F32)

    loop(bins // 2, clear_sums)

    def take(place):
        label_copy(place).wait_recv()
        forward_label_copy(place).start()
        data_copy(place).wait_recv()
        forward_copy(place).start()

    def arrived(place):
        forward_label_copy(place).wait_recv()
        forward_copy(place).wait_recv()

    def tile(side, lab, left, right):
        left_rows = side[pl.ds(2 * left, 2), :cap, :].reshape(2 * cap, width)
        left_lab = jnp.concatenate(
            [lab[2 * left + half].T[:cap, 0:1] for half in range(2)], axis=0)
        right_rows = own[pl.ds(2 * right, 2)].reshape(2 * LANES, width)
        right_lab = jnp.concatenate(
            [own_lab[2 * right + half, 0:1, :] for half in range(2)], axis=1)
        cosine = lax.dot_general(left_rows, right_rows, NT, preferred_element_type=F32)
        same = left_lab == right_lab
        dens = jnp.where(same, jnp.exp(cosine * (1.0 / SOFTMAX_TEMP)), 0.0)
        cent = jnp.where(same, cosine, 0.0)
        acc_dens[right] += jnp.sum(dens.reshape(2 * cap // 8, 8, 2 * LANES), axis=0)
        acc_cent[right] += jnp.sum(cent.reshape(2 * cap // 8, 8, 2 * LANES), axis=0)

    def close(pair):
        dens = jnp.sum(acc_dens[pair], axis=0, keepdims=True)
        cent = jnp.sum(acc_cent[pair], axis=0, keepdims=True)
        for half in range(2):
            part = slice(half * LANES, (half + 1) * LANES)
            ret[2 * pair + half] = jnp.concatenate(
                [dens[:, part], cent[:, part], jnp.zeros((6, LANES), F32)], axis=0)

    def span(count, body):
        if isinstance(count, int):
            loop(count, body)
        else:
            lax.fori_loop(0, count, lambda step, carry: (body(step), carry)[1], 0)

    def group(pair):
        span(pair, lambda q: tile(own, own_lab, pair, q))
        span(pair, lambda q: tile(own, own_lab, q, pair))
        tile(own, own_lab, pair, pair)
        span(pair, lambda q: tile(other, other_lab, q, pair))
        arrived(2 * pair)
        arrived(2 * pair + 1)

    def finish_group(pair):
        span(pair, lambda q: tile(other, other_lab, pair, q))
        tile(other, other_lab, pair, pair)

    pairs = bins // 2
    take(1)
    group(0)
    finish_group(0)

    def middle(s):
        take(2 * s + 2)
        take(2 * s + 3)
        group(s + 1)
        finish_group(s + 1)

    loop(pairs - 2, middle)
    last = pairs - 1
    take(2 * last)
    take(2 * last + 1)
    group(last)
    tile(other, other_lab, last, 0)
    close(0)
    ret_in[0] = ret[0]
    return_copy(1).start()

    def answer(s):
        tile(other, other_lab, last, s + 1)
        close(s + 1)
        return_copy(2 * s + 2).start()
        return_copy(2 * s + 3).start()

    loop(pairs - 1, answer)

    def gathered(place, total):
        values = ret_in[place].T
        mine = hot(place)
        return (total[0] + jnp.where(mine, values[:, 0:1], 0.0),
                total[1] + jnp.where(mine, values[:, 1:2], 0.0))

    none = jnp.zeros((LANES, rows), F32)
    total = gathered(0, (none, none))

    def collect(place, total):
        return_copy(place).wait_recv()
        return gathered(place, total)

    if bins <= 8:
        for place in range(1, bins):
            total = collect(place, total)
    else:
        total = lax.fori_loop(1, bins, collect, total)
    dens = jnp.sum(total[0], axis=0, keepdims=True) / size_row
    cent = jnp.sum(total[1], axis=0, keepdims=True) / size_row
    out_ref[...] = jnp.concatenate([jnp.log(dens), cent, jnp.zeros((6, rows), F32)], axis=0)

    def finish(s):
        data_copy(s + 1).wait_send()
        label_copy(s + 1).wait_send()
        return_copy(s + 1).wait_send()

    loop(bins - 1, finish)

    def finish_forward(s):
        forward_copy(s).wait_send()
        forward_label_copy(s).wait_send()

    loop(bins, finish_forward)


def on_device(embeddings, cluster_ids, cluster_sizes):
    n = lax.axis_size("blk")
    rows, width = embeddings.shape
    bins = n // 2
    total = rows * n
    limit = max(2 * total // bins, total * 5 // 32)
    cap = -(-(-(-limit // n)) // 16) * 16
    vmem = pl.BlockSpec(memory_space=pltpu.VMEM)
    hbm = pl.BlockSpec(memory_space=pltpu.HBM)
    dma = pltpu.SemaphoreType.DMA((bins,))
    out = pl.pallas_call(
        functools.partial(kernel, n, cap, float(limit)),
        out_shape=jax.ShapeDtypeStruct((8, rows), F32),
        in_specs=[hbm] * 3,
        out_specs=vmem,
        scratch_shapes=[
            pltpu.VMEM((rows, width), BF16),
            pltpu.VMEM(cluster_ids.shape, jnp.int32),
            pltpu.VMEM(cluster_sizes.shape, jnp.int32),
            pltpu.VMEM((bins, LANES, width), BF16),
            pltpu.VMEM((bins, 8, LANES), F32),
            pltpu.VMEM((bins, LANES, width), BF16),
            pltpu.VMEM((bins, LANES, width), BF16),
            pltpu.VMEM((bins, 8, LANES), F32),
            pltpu.VMEM((bins, 8, LANES), F32),
            pltpu.VMEM((bins, 8, LANES), F32),
            pltpu.VMEM((bins, 8, LANES), F32),
            pltpu.VMEM((8, rows), jnp.int32),
            pltpu.VMEM((bins // 2, 8, 2 * LANES), F32),
            pltpu.VMEM((bins // 2, 8, 2 * LANES), F32),
            pltpu.SemaphoreType.DMA,
            pltpu.SemaphoreType.DMA,
            pltpu.SemaphoreType.DMA,
        ] + [dma] * 10,
        compiler_params=pltpu.CompilerParams(
            collective_id=0, has_side_effects=True, vmem_limit_bytes=48 * 1024 * 1024),
        cost_estimate=pl.CostEstimate(flops=4 * 10 ** 9, bytes_accessed=10 ** 6, transcendentals=0),
    )(embeddings, cluster_ids, cluster_sizes)
    return out[0], out[1]


def solution(mesh):
    in_specs = (P(("groups", "blk"), None), P(("groups", "blk")), P("groups"))
    out_specs = (P(("groups", "blk")), P(("groups", "blk")))
    return jax.shard_map(
        on_device, mesh=mesh, in_specs=in_specs, out_specs=out_specs, check_vma=False
    )
```

```python
import functools

import jax
import jax.numpy as jnp
from jax import lax
from jax.experimental import pallas as pl
from jax.experimental.pallas import tpu as pltpu
from jax.sharding import PartitionSpec as P

SOFTMAX_TEMP = 0.1
EPSILON = 1e-06
LANES = 128
MESH = pl.DeviceIdType.MESH
F32 = jnp.float32
BF16 = jnp.bfloat16
NT = (((1,), (1,)), ((), ()))


def iota(shape, dim):
    return lax.broadcasted_iota(jnp.int32, shape, dim)


def loop(count, body):
    if count <= 8:
        for step in range(count):
            body(step)
    else:
        lax.fori_loop(0, count, lambda step, carry: (body(step), carry)[1], 0)


def kernel(n, cap, caps, chips, limit, emb_hbm, ids_hbm, sizes_hbm, out_ref,
           emb, ids_ref, sizes_ref, packed, packed_lab, own, other, own_lab, other_lab, ret, ret_in, addr_ref,
           acc_dens, acc_cent, emb_sem, ids_sem, sizes_sem,
           send, recv, send_lab, recv_lab, fsend, frecv, fsend_lab, frecv_lab, rsend, rrecv):
    bins = n // 2
    rows, width = emb.shape
    clusters = sizes_ref.shape[0]
    me = lax.axis_index("blk")
    chip = lax.div(me, 2)
    core = lax.rem(me, 2)
    partner = 2 * chip + 1 - core

    def distance(place):
        if isinstance(place, int) and place == 0:
            return 0
        return bins // 2 + (2 * lax.rem(place, 2) - 1) * lax.div(place, 2)

    def peer(place):
        return 2 * lax.rem(chip + distance(place), bins) + core

    def back(place):
        return 2 * lax.rem(chip + bins - distance(place), bins) + core

    fetch = pltpu.make_async_copy(emb_hbm, emb, emb_sem)
    fetch_ids = pltpu.make_async_copy(ids_hbm, ids_ref, ids_sem)
    fetch_sizes = pltpu.make_async_copy(sizes_hbm, sizes_ref, sizes_sem)
    fetch_sizes.start()
    fetch_ids.start()
    fetch.start()
    barrier = pltpu.get_barrier_semaphore()
    pl.semaphore_signal(barrier, inc=1, device_id={"blk": partner}, device_id_type=MESH)
    loop(bins - 1, lambda s: pl.semaphore_signal(
        barrier, inc=1, device_id={"blk": peer(s + 1)}, device_id_type=MESH))

    fetch_sizes.wait()
    sizes_row = sizes_ref[...].reshape(1, clusters).astype(F32)
    above = iota((clusters, clusters), 0)
    along = iota((clusters, clusters), 1)
    ends = jnp.sum(jnp.where(along <= above, sizes_row, 0.0), axis=1, keepdims=True)
    sizes = jnp.sum(jnp.where(along == above, sizes_row, 0.0), axis=1, keepdims=True)
    starts = ends - sizes
    shown = max(bins, 8)
    edge = jnp.zeros((1, 1), F32)
    bin_of = jnp.zeros((clusters, 1), F32)
    load = jnp.zeros((shown, 1), F32)
    load_row = jnp.zeros((1, LANES), F32)
    for index in range(bins):
        filled = edge
        edge = jnp.max(jnp.where(ends <= edge + limit, ends, 0.0), axis=0, keepdims=True)
        bin_of += jnp.where(starts >= edge, 1.0, 0.0)
        load = jnp.where(iota((shown, 1), 0) == index, edge - filled, load)
        load_row = jnp.where(iota((1, LANES), 1) == index, edge - filled, load_row)
    earlier = iota((shown, LANES), 1) < iota((shown, LANES), 0)
    ahead = (load_row > load) | ((load_row == load) & earlier)
    ahead = ahead & (iota((shown, LANES), 1) < bins)
    order = jnp.sum(jnp.where(ahead, 1.0, 0.0), axis=1, keepdims=True)
    home = jnp.zeros((shown, 1), F32)
    for place in range(bins):
        home = jnp.where(order == place, float(chips[place]), home)

    fetch_ids.wait()
    ids = ids_ref[...].reshape(1, rows)
    member = iota((clusters, rows), 0) == ids
    bin_row = jnp.sum(jnp.where(member, bin_of, 0.0), axis=0, keepdims=True)
    size_row = jnp.sum(jnp.where(member, sizes, 0.0), axis=0, keepdims=True)
    in_bin = iota((shown, rows), 0).astype(F32) == bin_row
    before = jnp.where(iota((rows, rows), 0) < iota((rows, rows), 1), 1.0, 0.0).astype(BF16)
    rank = jnp.dot(jnp.where(in_bin, 1.0, 0.0).astype(BF16), before, preferred_element_type=F32)
    slot = jnp.sum(jnp.where(in_bin, rank, 0.0), axis=0, keepdims=True)
    home_row = jnp.sum(jnp.where(in_bin, home, 0.0), axis=0, keepdims=True)
    address = (home_row * LANES + slot).astype(jnp.int32)
    addr_ref[...] = jnp.broadcast_to(address, addr_ref.shape)
    label_rows = jnp.broadcast_to((ids + 1).astype(F32), (8, rows)).astype(BF16)

    fetch.wait()
    values = emb[...].astype(F32)
    scale = lax.rsqrt(jnp.mean(values * values, axis=1, keepdims=True) + EPSILON)
    unit = (values * (scale * width ** (-0.5))).astype(BF16)

    def hot(place):
        first = lax.rem(chip + distance(place), bins) * LANES
        return iota((LANES, rows), 0) + first == addr_ref[0:1, :]

    def sized(where, act):
        for size in sorted(set(caps)):
            match = functools.reduce(
                jnp.logical_or, [where == chips[r] for r in range(bins) if caps[r] == size])
            pl.when(match)(functools.partial(act, size))

    def data_copy(place, size):
        return pltpu.make_async_remote_copy(
            packed.at[place, pl.ds(0, size)], own.at[place, pl.ds(0, size)],
            send.at[place], recv.at[place], device_id={"blk": peer(place)}, device_id_type=MESH)

    def label_copy(place):
        return pltpu.make_async_remote_copy(
            packed_lab.at[place], own_lab.at[place], send_lab.at[place], recv_lab.at[place],
            device_id={"blk": peer(place)}, device_id_type=MESH)

    def forward_copy(place, size):
        return pltpu.make_async_remote_copy(
            own.at[place, pl.ds(0, size)], other.at[place, pl.ds(0, size)],
            fsend.at[place], frecv.at[place], device_id={"blk": partner}, device_id_type=MESH)

    def forward_label_copy(place):
        return pltpu.make_async_remote_copy(
            own_lab.at[place], other_lab.at[place], fsend_lab.at[place], frecv_lab.at[place],
            device_id={"blk": partner}, device_id_type=MESH)

    def return_copy(place):
        return pltpu.make_async_remote_copy(
            ret.at[place], ret_in.at[place], rsend.at[place], rrecv.at[place],
            device_id={"blk": back(place)}, device_id_type=MESH)

    def pack(place, rows_ref, lab_ref):
        one_hot = jnp.where(hot(place), 1.0, 0.0).astype(BF16)
        rows_ref[place] = jnp.dot(one_hot, unit, preferred_element_type=F32).astype(BF16)
        lab_ref[place] = lax.dot_general(label_rows, one_hot, NT, preferred_element_type=F32)

    pl.semaphore_wait(barrier, bins)

    def send_step(s):
        pack(s + 1, packed, packed_lab)
        label_copy(s + 1).start()
        sized(lax.div(peer(s + 1), 2), lambda size: data_copy(s + 1, size).start())

    loop(bins - 1, send_step)
    pack(0, own, own_lab)
    forward_label_copy(0).start()
    sized(chip, lambda size: forward_copy(0, size).start())

    def clear(size):
        def step(s):
            if size < LANES:
                own[s + 1, size:, :] = jnp.zeros((LANES - size, width), BF16)
            if size < cap:
                other[s, size:cap, :] = jnp.zeros((cap - size, width), BF16)
        loop(bins - 1, step)
        if size < cap:
            other[bins - 1, size:cap, :] = jnp.zeros((cap - size, width), BF16)

    sized(chip, clear)

    def clear_sums(pair):
        acc_dens[pair] = jnp.zeros((8, 2 * LANES), F32)
        acc_cent[pair] = jnp.zeros((8, 2 * LANES), F32)

    loop(bins // 2, clear_sums)

    def take(place):
        label_copy(place).wait_recv()
        forward_label_copy(place).start()

        def go(size):
            data_copy(place, size).wait_recv()
            forward_copy(place, size).start()

        sized(chip, go)

    def arrived(place):
        forward_label_copy(place).wait_recv()
        sized(chip, lambda size: forward_copy(place, size).wait_recv())

    def tile(side, lab, left, right):
        left_rows = side[pl.ds(2 * left, 2), :cap, :].reshape(2 * cap, width)
        left_lab = jnp.concatenate(
            [lab[2 * left + half].T[:cap, 0:1] for half in range(2)], axis=0)
        right_rows = own[pl.ds(2 * right, 2)].reshape(2 * LANES, width)
        right_lab = jnp.concatenate(
            [own_lab[2 * right + half, 0:1, :] for half in range(2)], axis=1)
        cosine = lax.dot_general(left_rows, right_rows, NT, preferred_element_type=F32)
        same = left_lab == right_lab
        dens = jnp.where(same, jnp.exp(cosine * (1.0 / SOFTMAX_TEMP)), 0.0)
        cent = jnp.where(same, cosine, 0.0)
        acc_dens[right] += jnp.sum(dens.reshape(2 * cap // 8, 8, 2 * LANES), axis=0)
        acc_cent[right] += jnp.sum(cent.reshape(2 * cap // 8, 8, 2 * LANES), axis=0)

    def close(pair):
        dens = jnp.sum(acc_dens[pair], axis=0, keepdims=True)
        cent = jnp.sum(acc_cent[pair], axis=0, keepdims=True)
        for half in range(2):
            part = slice(half * LANES, (half + 1) * LANES)
            ret[2 * pair + half] = jnp.concatenate(
                [dens[:, part], cent[:, part], jnp.zeros((6, LANES), F32)], axis=0)

    def span(count, body):
        if isinstance(count, int):
            loop(count, body)
        else:
            lax.fori_loop(0, count, lambda step, carry: (body(step), carry)[1], 0)

    def group(pair):
        span(pair, lambda q: tile(own, own_lab, pair, q))
        span(pair, lambda q: tile(own, own_lab, q, pair))
        tile(own, own_lab, pair, pair)
        span(pair, lambda q: tile(other, other_lab, q, pair))
        arrived(2 * pair)
        arrived(2 * pair + 1)

    def finish_group(pair):
        span(pair, lambda q: tile(other, other_lab, pair, q))
        tile(other, other_lab, pair, pair)

    pairs = bins // 2
    take(1)
    group(0)
    finish_group(0)

    def middle(s):
        take(2 * s + 2)
        take(2 * s + 3)
        group(s + 1)
        finish_group(s + 1)

    loop(pairs - 2, middle)
    last = pairs - 1
    take(2 * last)
    take(2 * last + 1)
    group(last)
    tile(other, other_lab, last, 0)
    close(0)
    ret_in[0] = ret[0]
    return_copy(1).start()

    def answer(s):
        tile(other, other_lab, last, s + 1)
        close(s + 1)
        return_copy(2 * s + 2).start()
        return_copy(2 * s + 3).start()

    loop(pairs - 1, answer)

    def gathered(place, total):
        values = ret_in[place].T
        mine = hot(place)
        return (total[0] + jnp.where(mine, values[:, 0:1], 0.0),
                total[1] + jnp.where(mine, values[:, 1:2], 0.0))

    none = jnp.zeros((LANES, rows), F32)
    total = gathered(0, (none, none))

    def collect(place, total):
        return_copy(place).wait_recv()
        return gathered(place, total)

    if bins <= 8:
        for place in range(1, bins):
            total = collect(place, total)
    else:
        total = lax.fori_loop(1, bins, collect, total)
    dens = jnp.sum(total[0], axis=0, keepdims=True) / size_row
    cent = jnp.sum(total[1], axis=0, keepdims=True) / size_row
    out_ref[...] = jnp.concatenate([jnp.log(dens), cent, jnp.zeros((6, rows), F32)], axis=0)

    def finish(s):
        sized(lax.div(peer(s + 1), 2), lambda size: data_copy(s + 1, size).wait_send())
        label_copy(s + 1).wait_send()
        return_copy(s + 1).wait_send()

    loop(bins - 1, finish)

    def finish_forward(s):
        sized(chip, lambda size: forward_copy(s, size).wait_send())
        forward_label_copy(s).wait_send()

    loop(bins, finish_forward)


def on_device(embeddings, cluster_ids, cluster_sizes):
    n = lax.axis_size("blk")
    rows, width = embeddings.shape
    bins = n // 2
    total = rows * n
    limit = max(2 * total // bins, total * 5 // 32)
    caps = [-(-min(-(-limit // n), -(-rows // (r + 1))) // 16) * 16 for r in range(bins)]
    cap = caps[0]
    chips = []
    for r in range(bins // 2):
        low, high = bins // 2 - 1 - r, bins // 2 + r
        chips += [low, high] if r % 2 == 0 else [high, low]
    vmem = pl.BlockSpec(memory_space=pltpu.VMEM)
    hbm = pl.BlockSpec(memory_space=pltpu.HBM)
    dma = pltpu.SemaphoreType.DMA((bins,))
    out = pl.pallas_call(
        functools.partial(kernel, n, cap, tuple(caps), tuple(chips), float(limit)),
        out_shape=jax.ShapeDtypeStruct((8, rows), F32),
        in_specs=[hbm] * 3,
        out_specs=vmem,
        scratch_shapes=[
            pltpu.VMEM((rows, width), BF16),
            pltpu.VMEM(cluster_ids.shape, jnp.int32),
            pltpu.VMEM(cluster_sizes.shape, jnp.int32),
            pltpu.VMEM((bins, LANES, width), BF16),
            pltpu.VMEM((bins, 8, LANES), F32),
            pltpu.VMEM((bins, LANES, width), BF16),
            pltpu.VMEM((bins, LANES, width), BF16),
            pltpu.VMEM((bins, 8, LANES), F32),
            pltpu.VMEM((bins, 8, LANES), F32),
            pltpu.VMEM((bins, 8, LANES), F32),
            pltpu.VMEM((bins, 8, LANES), F32),
            pltpu.VMEM((8, rows), jnp.int32),
            pltpu.VMEM((bins // 2, 8, 2 * LANES), F32),
            pltpu.VMEM((bins // 2, 8, 2 * LANES), F32),
            pltpu.SemaphoreType.DMA,
            pltpu.SemaphoreType.DMA,
            pltpu.SemaphoreType.DMA,
        ] + [dma] * 10,
        compiler_params=pltpu.CompilerParams(
            collective_id=0, has_side_effects=True, vmem_limit_bytes=64 * 1024 * 1024 - 128 * 1024),
        cost_estimate=pl.CostEstimate(flops=4 * 10 ** 9, bytes_accessed=10 ** 6, transcendentals=0),
    )(embeddings, cluster_ids, cluster_sizes)
    return out[0], out[1]


def solution(mesh):
    in_specs = (P(("groups", "blk"), None), P(("groups", "blk")), P("groups"))
    out_specs = (P(("groups", "blk")), P(("groups", "blk")))
    return jax.shard_map(
        on_device, mesh=mesh, in_specs=in_specs, out_specs=out_specs, check_vma=False
    )
```

```python
import functools

import jax
import jax.numpy as jnp
from jax import lax
from jax.experimental import pallas as pl
from jax.experimental.pallas import tpu as pltpu
from jax.sharding import PartitionSpec as P

SOFTMAX_TEMP = 0.1
EPSILON = 1e-06
LANES = 128
MESH = pl.DeviceIdType.MESH
F32 = jnp.float32
BF16 = jnp.bfloat16
NT = (((1,), (1,)), ((), ()))


def iota(shape, dim):
    return lax.broadcasted_iota(jnp.int32, shape, dim)


def loop(count, body):
    if count <= 8:
        for step in range(count):
            body(step)
    else:
        lax.fori_loop(0, count, lambda step, carry: (body(step), carry)[1], 0)


def kernel(n, cap, caps, chips, limit, emb_hbm, ids_hbm, sizes_hbm, out_ref,
           emb, ids_ref, sizes_ref, packed, packed_lab, own, other, own_lab, other_lab, ret, ret_in, addr_ref,
           acc_dens, acc_cent, emb_sem, ids_sem, sizes_sem,
           send, recv, send_lab, recv_lab, fsend, frecv, fsend_lab, frecv_lab, rsend, rrecv):
    bins = n // 2
    rows, width = emb.shape
    clusters = sizes_ref.shape[0]
    me = lax.axis_index("blk")
    chip = lax.div(me, 2)
    core = lax.rem(me, 2)
    partner = 2 * chip + 1 - core

    def distance(place):
        if isinstance(place, int) and place == 0:
            return 0
        turn = bins - place
        return bins // 2 + (2 * lax.rem(turn, 2) - 1) * lax.div(turn, 2)

    def peer(place):
        return 2 * lax.rem(chip + distance(place), bins) + core

    def back(place):
        return 2 * lax.rem(chip + bins - distance(place), bins) + core

    fetch = pltpu.make_async_copy(emb_hbm, emb, emb_sem)
    fetch_ids = pltpu.make_async_copy(ids_hbm, ids_ref, ids_sem)
    fetch_sizes = pltpu.make_async_copy(sizes_hbm, sizes_ref, sizes_sem)
    fetch_sizes.start()
    fetch_ids.start()
    fetch.start()
    barrier = pltpu.get_barrier_semaphore()
    pl.semaphore_signal(barrier, inc=1, device_id={"blk": partner}, device_id_type=MESH)
    loop(bins - 1, lambda s: pl.semaphore_signal(
        barrier, inc=1, device_id={"blk": peer(s + 1)}, device_id_type=MESH))

    fetch_sizes.wait()
    sizes_row = sizes_ref[...].reshape(1, clusters).astype(F32)
    above = iota((clusters, clusters), 0)
    along = iota((clusters, clusters), 1)
    ends = jnp.sum(jnp.where(along <= above, sizes_row, 0.0), axis=1, keepdims=True)
    sizes = jnp.sum(jnp.where(along == above, sizes_row, 0.0), axis=1, keepdims=True)
    starts = ends - sizes
    shown = max(bins, 8)
    edge = jnp.zeros((1, 1), F32)
    bin_of = jnp.zeros((clusters, 1), F32)
    load = jnp.zeros((shown, 1), F32)
    load_row = jnp.zeros((1, LANES), F32)
    for index in range(bins):
        filled = edge
        edge = jnp.max(jnp.where(ends <= edge + limit, ends, 0.0), axis=0, keepdims=True)
        bin_of += jnp.where(starts >= edge, 1.0, 0.0)
        load = jnp.where(iota((shown, 1), 0) == index, edge - filled, load)
        load_row = jnp.where(iota((1, LANES), 1) == index, edge - filled, load_row)
    earlier = iota((shown, LANES), 1) < iota((shown, LANES), 0)
    ahead = (load_row > load) | ((load_row == load) & earlier)
    ahead = ahead & (iota((shown, LANES), 1) < bins)
    order = jnp.sum(jnp.where(ahead, 1.0, 0.0), axis=1, keepdims=True)
    home = jnp.zeros((shown, 1), F32)
    for place in range(bins):
        home = jnp.where(order == place, float(chips[place]), home)

    fetch_ids.wait()
    ids = ids_ref[...].reshape(1, rows)
    member = iota((clusters, rows), 0) == ids
    bin_row = jnp.sum(jnp.where(member, bin_of, 0.0), axis=0, keepdims=True)
    size_row = jnp.sum(jnp.where(member, sizes, 0.0), axis=0, keepdims=True)
    in_bin = iota((shown, rows), 0).astype(F32) == bin_row
    before = jnp.where(iota((rows, rows), 0) < iota((rows, rows), 1), 1.0, 0.0).astype(BF16)
    rank = jnp.dot(jnp.where(in_bin, 1.0, 0.0).astype(BF16), before, preferred_element_type=F32)
    slot = jnp.sum(jnp.where(in_bin, rank, 0.0), axis=0, keepdims=True)
    home_row = jnp.sum(jnp.where(in_bin, home, 0.0), axis=0, keepdims=True)
    address = (home_row * LANES + slot).astype(jnp.int32)
    addr_ref[...] = jnp.broadcast_to(address, addr_ref.shape)
    label_rows = jnp.broadcast_to((ids + 1).astype(F32), (8, rows)).astype(BF16)

    fetch.wait()
    values = emb[...].astype(F32)
    scale = lax.rsqrt(jnp.mean(values * values, axis=1, keepdims=True) + EPSILON)
    unit = (values * (scale * width ** (-0.5))).astype(BF16)

    def hot(place):
        first = lax.rem(chip + distance(place), bins) * LANES
        return iota((LANES, rows), 0) + first == addr_ref[0:1, :]

    def sized(where, act):
        for size in sorted(set(caps)):
            match = functools.reduce(
                jnp.logical_or, [where == chips[r] for r in range(bins) if caps[r] == size])
            pl.when(match)(functools.partial(act, size))

    def data_copy(place, size):
        return pltpu.make_async_remote_copy(
            packed.at[place, pl.ds(0, size)], own.at[place, pl.ds(0, size)],
            send.at[place], recv.at[place], device_id={"blk": peer(place)}, device_id_type=MESH)

    def label_copy(place):
        return pltpu.make_async_remote_copy(
            packed_lab.at[place], own_lab.at[place], send_lab.at[place], recv_lab.at[place],
            device_id={"blk": peer(place)}, device_id_type=MESH)

    def forward_copy(place, size):
        return pltpu.make_async_remote_copy(
            own.at[place, pl.ds(0, size)], other.at[place, pl.ds(0, size)],
            fsend.at[place], frecv.at[place], device_id={"blk": partner}, device_id_type=MESH)

    def forward_label_copy(place):
        return pltpu.make_async_remote_copy(
            own_lab.at[place], other_lab.at[place], fsend_lab.at[place], frecv_lab.at[place],
            device_id={"blk": partner}, device_id_type=MESH)

    def return_copy(place):
        return pltpu.make_async_remote_copy(
            ret.at[place], ret_in.at[place], rsend.at[place], rrecv.at[place],
            device_id={"blk": back(place)}, device_id_type=MESH)

    def pack(place, rows_ref, lab_ref):
        one_hot = jnp.where(hot(place), 1.0, 0.0).astype(BF16)
        rows_ref[place] = jnp.dot(one_hot, unit, preferred_element_type=F32).astype(BF16)
        lab_ref[place] = lax.dot_general(label_rows, one_hot, NT, preferred_element_type=F32)

    pl.semaphore_wait(barrier, bins)

    def send_step(s):
        place = bins - 1 - s
        pack(place, packed, packed_lab)
        label_copy(place).start()
        sized(lax.div(peer(place), 2), lambda size: data_copy(place, size).start())

    loop(bins - 1, send_step)
    pack(0, own, own_lab)
    forward_label_copy(0).start()
    sized(chip, lambda size: forward_copy(0, size).start())

    def clear(size):
        def step(s):
            if size < LANES:
                own[s + 1, size:, :] = jnp.zeros((LANES - size, width), BF16)
            if size < cap:
                other[s, size:cap, :] = jnp.zeros((cap - size, width), BF16)
        loop(bins - 1, step)
        if size < cap:
            other[bins - 1, size:cap, :] = jnp.zeros((cap - size, width), BF16)

    sized(chip, clear)

    def clear_sums(pair):
        acc_dens[pair] = jnp.zeros((8, 2 * LANES), F32)
        acc_cent[pair] = jnp.zeros((8, 2 * LANES), F32)

    loop(bins // 2, clear_sums)

    def take(place):
        label_copy(place).wait_recv()
        forward_label_copy(place).start()

        def go(size):
            data_copy(place, size).wait_recv()
            forward_copy(place, size).start()

        sized(chip, go)

    def arrived(place):
        forward_label_copy(place).wait_recv()
        sized(chip, lambda size: forward_copy(place, size).wait_recv())

    def tile(side, lab, left, right):
        left_rows = side[pl.ds(2 * left, 2), :cap, :].reshape(2 * cap, width)
        left_lab = jnp.concatenate(
            [lab[2 * left + half].T[:cap, 0:1] for half in range(2)], axis=0)
        right_rows = own[pl.ds(2 * right, 2)].reshape(2 * LANES, width)
        right_lab = jnp.concatenate(
            [own_lab[2 * right + half, 0:1, :] for half in range(2)], axis=1)
        cosine = lax.dot_general(left_rows, right_rows, NT, preferred_element_type=F32)
        same = left_lab == right_lab
        dens = jnp.where(same, jnp.exp(cosine * (1.0 / SOFTMAX_TEMP)), 0.0)
        cent = jnp.where(same, cosine, 0.0)
        acc_dens[right] += jnp.sum(dens.reshape(2 * cap // 8, 8, 2 * LANES), axis=0)
        acc_cent[right] += jnp.sum(cent.reshape(2 * cap // 8, 8, 2 * LANES), axis=0)

    def close(pair):
        dens = jnp.sum(acc_dens[pair], axis=0, keepdims=True)
        cent = jnp.sum(acc_cent[pair], axis=0, keepdims=True)
        for half in range(2):
            part = slice(half * LANES, (half + 1) * LANES)
            ret[2 * pair + half] = jnp.concatenate(
                [dens[:, part], cent[:, part], jnp.zeros((6, LANES), F32)], axis=0)

    def span(count, body):
        if isinstance(count, int):
            loop(count, body)
        else:
            lax.fori_loop(0, count, lambda step, carry: (body(step), carry)[1], 0)

    def group(pair):
        span(pair, lambda q: tile(own, own_lab, pair, q))
        span(pair, lambda q: tile(own, own_lab, q, pair))
        tile(own, own_lab, pair, pair)
        span(pair, lambda q: tile(other, other_lab, q, pair))
        arrived(2 * pair)
        arrived(2 * pair + 1)

    def finish_group(pair):
        span(pair, lambda q: tile(other, other_lab, pair, q))
        tile(other, other_lab, pair, pair)

    pairs = bins // 2
    take(1)
    group(0)
    finish_group(0)

    def middle(s):
        take(2 * s + 2)
        take(2 * s + 3)
        group(s + 1)
        finish_group(s + 1)

    loop(pairs - 2, middle)
    last = pairs - 1
    take(2 * last)
    take(2 * last + 1)
    group(last)
    tile(other, other_lab, last, 0)
    close(0)
    ret_in[0] = ret[0]
    return_copy(1).start()

    def answer(s):
        tile(other, other_lab, last, s + 1)
        close(s + 1)
        return_copy(2 * s + 2).start()
        return_copy(2 * s + 3).start()

    loop(pairs - 1, answer)

    def gathered(place, total):
        values = ret_in[place].T
        mine = hot(place)
        return (total[0] + jnp.where(mine, values[:, 0:1], 0.0),
                total[1] + jnp.where(mine, values[:, 1:2], 0.0))

    none = jnp.zeros((LANES, rows), F32)
    total = gathered(0, (none, none))

    def collect(place, total):
        return_copy(place).wait_recv()
        return gathered(place, total)

    if bins <= 8:
        for place in range(1, bins):
            total = collect(place, total)
    else:
        total = lax.fori_loop(1, bins, collect, total)
    dens = jnp.sum(total[0], axis=0, keepdims=True) / size_row
    cent = jnp.sum(total[1], axis=0, keepdims=True) / size_row
    out_ref[...] = jnp.concatenate([jnp.log(dens), cent, jnp.zeros((6, rows), F32)], axis=0)

    def finish(s):
        sized(lax.div(peer(s + 1), 2), lambda size: data_copy(s + 1, size).wait_send())
        label_copy(s + 1).wait_send()
        return_copy(s + 1).wait_send()

    loop(bins - 1, finish)

    def finish_forward(s):
        sized(chip, lambda size: forward_copy(s, size).wait_send())
        forward_label_copy(s).wait_send()

    loop(bins, finish_forward)


def on_device(embeddings, cluster_ids, cluster_sizes):
    n = lax.axis_size("blk")
    rows, width = embeddings.shape
    bins = n // 2
    total = rows * n
    limit = max(2 * total // bins, total * 5 // 32)
    caps = [-(-min(-(-limit // n), -(-rows // (r + 1))) // 16) * 16 for r in range(bins)]
    cap = caps[0]
    chips = []
    for r in range(bins // 2):
        low, high = bins // 2 - 1 - r, bins // 2 + r
        chips += [low, high] if r % 2 == 0 else [high, low]
    vmem = pl.BlockSpec(memory_space=pltpu.VMEM)
    hbm = pl.BlockSpec(memory_space=pltpu.HBM)
    dma = pltpu.SemaphoreType.DMA((bins,))
    out = pl.pallas_call(
        functools.partial(kernel, n, cap, tuple(caps), tuple(chips), float(limit)),
        out_shape=jax.ShapeDtypeStruct((8, rows), F32),
        in_specs=[hbm] * 3,
        out_specs=vmem,
        scratch_shapes=[
            pltpu.VMEM((rows, width), BF16),
            pltpu.VMEM(cluster_ids.shape, jnp.int32),
            pltpu.VMEM(cluster_sizes.shape, jnp.int32),
            pltpu.VMEM((bins, LANES, width), BF16),
            pltpu.VMEM((bins, 8, LANES), F32),
            pltpu.VMEM((bins, LANES, width), BF16),
            pltpu.VMEM((bins, LANES, width), BF16),
            pltpu.VMEM((bins, 8, LANES), F32),
            pltpu.VMEM((bins, 8, LANES), F32),
            pltpu.VMEM((bins, 8, LANES), F32),
            pltpu.VMEM((bins, 8, LANES), F32),
            pltpu.VMEM((8, rows), jnp.int32),
            pltpu.VMEM((bins // 2, 8, 2 * LANES), F32),
            pltpu.VMEM((bins // 2, 8, 2 * LANES), F32),
            pltpu.SemaphoreType.DMA,
            pltpu.SemaphoreType.DMA,
            pltpu.SemaphoreType.DMA,
        ] + [dma] * 10,
        compiler_params=pltpu.CompilerParams(
            collective_id=0, has_side_effects=True, vmem_limit_bytes=64 * 1024 * 1024 - 128 * 1024),
        cost_estimate=pl.CostEstimate(flops=4 * 10 ** 9, bytes_accessed=10 ** 6, transcendentals=0),
    )(embeddings, cluster_ids, cluster_sizes)
    return out[0], out[1]


def solution(mesh):
    in_specs = (P(("groups", "blk"), None), P(("groups", "blk")), P("groups"))
    out_specs = (P(("groups", "blk")), P(("groups", "blk")))
    return jax.shard_map(
        on_device, mesh=mesh, in_specs=in_specs, out_specs=out_specs, check_vma=False
    )
```

```python
import functools

import jax
import jax.numpy as jnp
from jax import lax
from jax.experimental import pallas as pl
from jax.experimental.pallas import tpu as pltpu
from jax.sharding import PartitionSpec as P

SOFTMAX_TEMP = 0.1
EPSILON = 1e-06
LANES = 128
MESH = pl.DeviceIdType.MESH
F32 = jnp.float32
BF16 = jnp.bfloat16
NT = (((1,), (1,)), ((), ()))


def iota(shape, dim):
    return lax.broadcasted_iota(jnp.int32, shape, dim)


def loop(count, body):
    if count <= 8:
        for step in range(count):
            body(step)
    else:
        lax.fori_loop(0, count, lambda step, carry: (body(step), carry)[1], 0)


def kernel(n, cap, caps, chips, limit, emb_hbm, ids_hbm, sizes_hbm, out_ref,
           emb, ids_ref, sizes_ref, packed, packed_lab, own, other, own_lab, other_lab, ret, ret_in, addr_ref,
           acc_dens, acc_cent, emb_sem, ids_sem, sizes_sem,
           send, recv, send_lab, recv_lab, fsend, frecv, fsend_lab, frecv_lab, rsend, rrecv):
    bins = n // 2
    rows, width = emb.shape
    clusters = sizes_ref.shape[0]
    me = lax.axis_index("blk")
    chip = lax.div(me, 2)
    core = lax.rem(me, 2)
    partner = 2 * chip + 1 - core

    def turn(place):
        if isinstance(place, int) and place == 0:
            return jnp.int32(0)
        place = jnp.int32(place)
        half = lax.div(place, 2)
        odd = lax.rem(place, 2)
        first = odd * (bins // 2 + half) + (1 - odd) * half
        second = odd * (half + 1) + (1 - odd) * (bins // 2 + half - 1)
        at_end = lax.div(place, bins - 1)
        second = at_end * (bins - 1) + (1 - at_end) * second
        return first + core * (second - first)

    def facing(place):
        change, other_chip, bit = turn(place), chip, 1
        while bit < bins:
            flip = lax.rem(lax.div(change, bit), 2)
            other_chip = other_chip + flip * bit * (1 - 2 * lax.rem(lax.div(chip, bit), 2))
            bit *= 2
        return other_chip

    def peer(place):
        return 2 * facing(place) + core

    fetch = pltpu.make_async_copy(emb_hbm, emb, emb_sem)
    fetch_ids = pltpu.make_async_copy(ids_hbm, ids_ref, ids_sem)
    fetch_sizes = pltpu.make_async_copy(sizes_hbm, sizes_ref, sizes_sem)
    fetch_sizes.start()
    fetch_ids.start()
    fetch.start()
    barrier = pltpu.get_barrier_semaphore()
    pl.semaphore_signal(barrier, inc=1, device_id={"blk": partner}, device_id_type=MESH)
    loop(bins - 1, lambda s: pl.semaphore_signal(
        barrier, inc=1, device_id={"blk": peer(s + 1)}, device_id_type=MESH))

    fetch_sizes.wait()
    sizes_row = sizes_ref[...].reshape(1, clusters).astype(F32)
    above = iota((clusters, clusters), 0)
    along = iota((clusters, clusters), 1)
    ends = jnp.sum(jnp.where(along <= above, sizes_row, 0.0), axis=1, keepdims=True)
    sizes = jnp.sum(jnp.where(along == above, sizes_row, 0.0), axis=1, keepdims=True)
    starts = ends - sizes
    shown = max(bins, 8)
    edge = jnp.zeros((1, 1), F32)
    bin_of = jnp.zeros((clusters, 1), F32)
    load = jnp.zeros((shown, 1), F32)
    load_row = jnp.zeros((1, LANES), F32)
    for index in range(bins):
        filled = edge
        edge = jnp.max(jnp.where(ends <= edge + limit, ends, 0.0), axis=0, keepdims=True)
        bin_of += jnp.where(starts >= edge, 1.0, 0.0)
        load = jnp.where(iota((shown, 1), 0) == index, edge - filled, load)
        load_row = jnp.where(iota((1, LANES), 1) == index, edge - filled, load_row)
    earlier = iota((shown, LANES), 1) < iota((shown, LANES), 0)
    ahead = (load_row > load) | ((load_row == load) & earlier)
    ahead = ahead & (iota((shown, LANES), 1) < bins)
    order = jnp.sum(jnp.where(ahead, 1.0, 0.0), axis=1, keepdims=True)
    home = jnp.zeros((shown, 1), F32)
    for place in range(bins):
        home = jnp.where(order == place, float(chips[place]), home)

    fetch_ids.wait()
    ids = ids_ref[...].reshape(1, rows)
    member = iota((clusters, rows), 0) == ids
    bin_row = jnp.sum(jnp.where(member, bin_of, 0.0), axis=0, keepdims=True)
    size_row = jnp.sum(jnp.where(member, sizes, 0.0), axis=0, keepdims=True)
    in_bin = iota((shown, rows), 0).astype(F32) == bin_row
    before = jnp.where(iota((rows, rows), 0) < iota((rows, rows), 1), 1.0, 0.0).astype(BF16)
    rank = jnp.dot(jnp.where(in_bin, 1.0, 0.0).astype(BF16), before, preferred_element_type=F32)
    slot = jnp.sum(jnp.where(in_bin, rank, 0.0), axis=0, keepdims=True)
    home_row = jnp.sum(jnp.where(in_bin, home, 0.0), axis=0, keepdims=True)
    address = (home_row * LANES + slot).astype(jnp.int32)
    addr_ref[...] = jnp.broadcast_to(address, addr_ref.shape)
    label_rows = jnp.broadcast_to((ids + 1).astype(F32), (8, rows)).astype(BF16)

    fetch.wait()
    values = emb[...].astype(F32)
    scale = lax.rsqrt(jnp.mean(values * values, axis=1, keepdims=True) + EPSILON)
    unit = (values * (scale * width ** (-0.5))).astype(BF16)

    def hot(place):
        first = facing(place) * LANES
        return iota((LANES, rows), 0) + first == addr_ref[0:1, :]

    def sized(where, act):
        for size in sorted(set(caps)):
            match = functools.reduce(
                jnp.logical_or, [where == chips[r] for r in range(bins) if caps[r] == size])
            pl.when(match)(functools.partial(act, size))

    def data_copy(place, size):
        return pltpu.make_async_remote_copy(
            packed.at[place, pl.ds(0, size)], own.at[place, pl.ds(0, size)],
            send.at[place], recv.at[place], device_id={"blk": peer(place)}, device_id_type=MESH)

    def label_copy(place):
        return pltpu.make_async_remote_copy(
            packed_lab.at[place], own_lab.at[place], send_lab.at[place], recv_lab.at[place],
            device_id={"blk": peer(place)}, device_id_type=MESH)

    def forward_copy(place, size):
        return pltpu.make_async_remote_copy(
            own.at[place, pl.ds(0, size)], other.at[place, pl.ds(0, size)],
            fsend.at[place], frecv.at[place], device_id={"blk": partner}, device_id_type=MESH)

    def forward_label_copy(place):
        return pltpu.make_async_remote_copy(
            own_lab.at[place], other_lab.at[place], fsend_lab.at[place], frecv_lab.at[place],
            device_id={"blk": partner}, device_id_type=MESH)

    def return_copy(place):
        return pltpu.make_async_remote_copy(
            ret.at[place], ret_in.at[place], rsend.at[place], rrecv.at[place],
            device_id={"blk": peer(place)}, device_id_type=MESH)

    def pack(place, rows_ref, lab_ref):
        one_hot = jnp.where(hot(place), 1.0, 0.0).astype(BF16)
        rows_ref[place] = jnp.dot(one_hot, unit, preferred_element_type=F32).astype(BF16)
        lab_ref[place] = lax.dot_general(label_rows, one_hot, NT, preferred_element_type=F32)

    pl.semaphore_wait(barrier, bins)

    def send_step(s):
        pack(s + 1, packed, packed_lab)
        label_copy(s + 1).start()
        sized(facing(s + 1), lambda size: data_copy(s + 1, size).start())

    loop(bins - 1, send_step)
    pack(0, own, own_lab)
    forward_label_copy(0).start()
    sized(chip, lambda size: forward_copy(0, size).start())

    def clear(size):
        def step(s):
            if size < LANES:
                own[s + 1, size:, :] = jnp.zeros((LANES - size, width), BF16)
            if size < cap:
                other[s, size:cap, :] = jnp.zeros((cap - size, width), BF16)
        loop(bins - 1, step)
        if size < cap:
            other[bins - 1, size:cap, :] = jnp.zeros((cap - size, width), BF16)

    sized(chip, clear)

    def clear_sums(pair):
        acc_dens[pair] = jnp.zeros((8, 2 * LANES), F32)
        acc_cent[pair] = jnp.zeros((8, 2 * LANES), F32)

    loop(bins // 2, clear_sums)

    def take(place):
        label_copy(place).wait_recv()
        forward_label_copy(place).start()

        def go(size):
            data_copy(place, size).wait_recv()
            forward_copy(place, size).start()

        sized(chip, go)

    def arrived(place):
        forward_label_copy(place).wait_recv()
        sized(chip, lambda size: forward_copy(place, size).wait_recv())

    def tile(side, lab, left, right):
        left_rows = side[pl.ds(2 * left, 2), :cap, :].reshape(2 * cap, width)
        left_lab = jnp.concatenate(
            [lab[2 * left + half].T[:cap, 0:1] for half in range(2)], axis=0)
        right_rows = own[pl.ds(2 * right, 2)].reshape(2 * LANES, width)
        right_lab = jnp.concatenate(
            [own_lab[2 * right + half, 0:1, :] for half in range(2)], axis=1)
        cosine = lax.dot_general(left_rows, right_rows, NT, preferred_element_type=F32)
        same = left_lab == right_lab
        dens = jnp.where(same, jnp.exp(cosine * (1.0 / SOFTMAX_TEMP)), 0.0)
        cent = jnp.where(same, cosine, 0.0)
        acc_dens[right] += jnp.sum(dens.reshape(2 * cap // 8, 8, 2 * LANES), axis=0)
        acc_cent[right] += jnp.sum(cent.reshape(2 * cap // 8, 8, 2 * LANES), axis=0)

    def close(pair):
        dens = jnp.sum(acc_dens[pair], axis=0, keepdims=True)
        cent = jnp.sum(acc_cent[pair], axis=0, keepdims=True)
        for half in range(2):
            part = slice(half * LANES, (half + 1) * LANES)
            ret[2 * pair + half] = jnp.concatenate(
                [dens[:, part], cent[:, part], jnp.zeros((6, LANES), F32)], axis=0)

    def span(count, body):
        if isinstance(count, int):
            loop(count, body)
        else:
            lax.fori_loop(0, count, lambda step, carry: (body(step), carry)[1], 0)

    def group(pair):
        span(pair, lambda q: tile(own, own_lab, pair, q))
        span(pair, lambda q: tile(own, own_lab, q, pair))
        tile(own, own_lab, pair, pair)
        span(pair, lambda q: tile(other, other_lab, q, pair))
        arrived(2 * pair)
        arrived(2 * pair + 1)

    def finish_group(pair):
        span(pair, lambda q: tile(other, other_lab, pair, q))
        tile(other, other_lab, pair, pair)

    pairs = bins // 2
    take(1)
    group(0)
    finish_group(0)

    def middle(s):
        take(2 * s + 2)
        take(2 * s + 3)
        group(s + 1)
        finish_group(s + 1)

    loop(pairs - 2, middle)
    last = pairs - 1
    take(2 * last)
    take(2 * last + 1)
    group(last)
    tile(other, other_lab, last, 0)
    close(0)
    ret_in[0] = ret[0]
    return_copy(1).start()

    def answer(s):
        tile(other, other_lab, last, s + 1)
        close(s + 1)
        return_copy(2 * s + 2).start()
        return_copy(2 * s + 3).start()

    loop(pairs - 1, answer)

    def gathered(place, total):
        values = ret_in[place].T
        mine = hot(place)
        return (total[0] + jnp.where(mine, values[:, 0:1], 0.0),
                total[1] + jnp.where(mine, values[:, 1:2], 0.0))

    none = jnp.zeros((LANES, rows), F32)
    total = gathered(0, (none, none))

    def collect(place, total):
        return_copy(place).wait_recv()
        return gathered(place, total)

    if bins <= 8:
        for place in range(1, bins):
            total = collect(place, total)
    else:
        total = lax.fori_loop(1, bins, collect, total)
    dens = jnp.sum(total[0], axis=0, keepdims=True) / size_row
    cent = jnp.sum(total[1], axis=0, keepdims=True) / size_row
    out_ref[...] = jnp.concatenate([jnp.log(dens), cent, jnp.zeros((6, rows), F32)], axis=0)

    def finish(s):
        sized(facing(s + 1), lambda size: data_copy(s + 1, size).wait_send())
        label_copy(s + 1).wait_send()
        return_copy(s + 1).wait_send()

    loop(bins - 1, finish)

    def finish_forward(s):
        sized(chip, lambda size: forward_copy(s, size).wait_send())
        forward_label_copy(s).wait_send()

    loop(bins, finish_forward)


def on_device(embeddings, cluster_ids, cluster_sizes):
    n = lax.axis_size("blk")
    rows, width = embeddings.shape
    bins = n // 2
    total = rows * n
    limit = max(2 * total // bins, total * 5 // 32)
    caps = [-(-min(-(-limit // n), -(-rows // (r + 1))) // 16) * 16 for r in range(bins)]
    cap = caps[0]
    chips = []
    for r in range(bins // 2):
        low, high = bins // 2 - 1 - r, bins // 2 + r
        chips += [low, high] if r % 2 == 0 else [high, low]
    vmem = pl.BlockSpec(memory_space=pltpu.VMEM)
    hbm = pl.BlockSpec(memory_space=pltpu.HBM)
    dma = pltpu.SemaphoreType.DMA((bins,))
    out = pl.pallas_call(
        functools.partial(kernel, n, cap, tuple(caps), tuple(chips), float(limit)),
        out_shape=jax.ShapeDtypeStruct((8, rows), F32),
        in_specs=[hbm] * 3,
        out_specs=vmem,
        scratch_shapes=[
            pltpu.VMEM((rows, width), BF16),
            pltpu.VMEM(cluster_ids.shape, jnp.int32),
            pltpu.VMEM(cluster_sizes.shape, jnp.int32),
            pltpu.VMEM((bins, LANES, width), BF16),
            pltpu.VMEM((bins, 8, LANES), F32),
            pltpu.VMEM((bins, LANES, width), BF16),
            pltpu.VMEM((bins, LANES, width), BF16),
            pltpu.VMEM((bins, 8, LANES), F32),
            pltpu.VMEM((bins, 8, LANES), F32),
            pltpu.VMEM((bins, 8, LANES), F32),
            pltpu.VMEM((bins, 8, LANES), F32),
            pltpu.VMEM((8, rows), jnp.int32),
            pltpu.VMEM((bins // 2, 8, 2 * LANES), F32),
            pltpu.VMEM((bins // 2, 8, 2 * LANES), F32),
            pltpu.SemaphoreType.DMA,
            pltpu.SemaphoreType.DMA,
            pltpu.SemaphoreType.DMA,
        ] + [dma] * 10,
        compiler_params=pltpu.CompilerParams(
            collective_id=0, has_side_effects=True, vmem_limit_bytes=64 * 1024 * 1024 - 128 * 1024),
        cost_estimate=pl.CostEstimate(flops=4 * 10 ** 9, bytes_accessed=10 ** 6, transcendentals=0),
    )(embeddings, cluster_ids, cluster_sizes)
    return out[0], out[1]


def solution(mesh):
    in_specs = (P(("groups", "blk"), None), P(("groups", "blk")), P("groups"))
    out_specs = (P(("groups", "blk")), P(("groups", "blk")))
    return jax.shard_map(
        on_device, mesh=mesh, in_specs=in_specs, out_specs=out_specs, check_vma=False
    )
```

```python
import functools

import jax
import jax.numpy as jnp
from jax import lax
from jax.experimental import pallas as pl
from jax.experimental.pallas import tpu as pltpu
from jax.sharding import PartitionSpec as P

SOFTMAX_TEMP = 0.1
EPSILON = 1e-06
LANES = 128
MESH = pl.DeviceIdType.MESH
F32 = jnp.float32
BF16 = jnp.bfloat16
NT = (((1,), (1,)), ((), ()))


def iota(shape, dim):
    return lax.broadcasted_iota(jnp.int32, shape, dim)


def loop(count, body):
    if count <= 8:
        for step in range(count):
            body(step)
    else:
        lax.fori_loop(0, count, lambda step, carry: (body(step), carry)[1], 0)


def kernel(n, cap, caps, chips, limit, emb_hbm, ids_hbm, sizes_hbm, out_ref,
           emb, ids_ref, sizes_ref, packed, packed_lab, own, other, own_lab, other_lab, ret, ret_in, addr_ref,
           acc_dens, acc_cent, before_ref, emb_sem, ids_sem, sizes_sem,
           send, recv, send_lab, recv_lab, fsend, frecv, fsend_lab, frecv_lab, rsend, rrecv):
    bins = n // 2
    rows, width = emb.shape
    clusters = sizes_ref.shape[0]
    me = lax.axis_index("blk")
    chip = lax.div(me, 2)
    core = lax.rem(me, 2)
    partner = 2 * chip + 1 - core

    def turn(place):
        if isinstance(place, int) and place == 0:
            return jnp.int32(0)
        place = jnp.int32(place)
        half = lax.div(place, 2)
        odd = lax.rem(place, 2)
        first = odd * (bins // 2 + half) + (1 - odd) * half
        second = odd * (half + 1) + (1 - odd) * (bins // 2 + half - 1)
        at_end = lax.div(place, bins - 1)
        second = at_end * (bins - 1) + (1 - at_end) * second
        return first + core * (second - first)

    def facing(place):
        change, other_chip, bit = turn(place), chip, 1
        while bit < bins:
            flip = lax.rem(lax.div(change, bit), 2)
            other_chip = other_chip + flip * bit * (1 - 2 * lax.rem(lax.div(chip, bit), 2))
            bit *= 2
        return other_chip

    def peer(place):
        return 2 * facing(place) + core

    fetch = pltpu.make_async_copy(emb_hbm, emb, emb_sem)
    fetch_ids = pltpu.make_async_copy(ids_hbm, ids_ref, ids_sem)
    fetch_sizes = pltpu.make_async_copy(sizes_hbm, sizes_ref, sizes_sem)
    fetch_sizes.start()
    fetch_ids.start()
    fetch.start()
    barrier = pltpu.get_barrier_semaphore()
    pl.semaphore_signal(barrier, inc=1, device_id={"blk": partner}, device_id_type=MESH)
    loop(bins - 1, lambda s: pl.semaphore_signal(
        barrier, inc=1, device_id={"blk": peer(s + 1)}, device_id_type=MESH))

    before_ref[...] = jnp.where(
        iota((rows, rows), 0) < iota((rows, rows), 1), 1.0, 0.0).astype(BF16)

    fetch_sizes.wait()
    sizes_row = sizes_ref[...].reshape(1, clusters).astype(F32)
    above = iota((clusters, clusters), 0)
    along = iota((clusters, clusters), 1)
    ends = jnp.sum(jnp.where(along <= above, sizes_row, 0.0), axis=1, keepdims=True)
    sizes = jnp.sum(jnp.where(along == above, sizes_row, 0.0), axis=1, keepdims=True)
    starts = ends - sizes
    shown = max(bins, 8)
    edge = jnp.zeros((1, 1), F32)
    bin_of = jnp.zeros((clusters, 1), F32)
    load = jnp.zeros((shown, 1), F32)
    load_row = jnp.zeros((1, LANES), F32)
    for index in range(bins):
        filled = edge
        edge = jnp.max(jnp.where(ends <= edge + limit, ends, 0.0), axis=0, keepdims=True)
        bin_of += jnp.where(starts >= edge, 1.0, 0.0)
        load = jnp.where(iota((shown, 1), 0) == index, edge - filled, load)
        load_row = jnp.where(iota((1, LANES), 1) == index, edge - filled, load_row)
    earlier = iota((shown, LANES), 1) < iota((shown, LANES), 0)
    ahead = (load_row > load) | ((load_row == load) & earlier)
    ahead = ahead & (iota((shown, LANES), 1) < bins)
    order = jnp.sum(jnp.where(ahead, 1.0, 0.0), axis=1, keepdims=True)
    home = jnp.zeros((shown, 1), F32)
    for place in range(bins):
        home = jnp.where(order == place, float(chips[place]), home)

    fetch_ids.wait()
    ids = ids_ref[...].reshape(1, rows)
    member = iota((clusters, rows), 0) == ids
    bin_row = jnp.sum(jnp.where(member, bin_of, 0.0), axis=0, keepdims=True)
    size_row = jnp.sum(jnp.where(member, sizes, 0.0), axis=0, keepdims=True)
    in_bin = iota((shown, rows), 0).astype(F32) == bin_row
    rank = jnp.dot(jnp.where(in_bin, 1.0, 0.0).astype(BF16), before_ref[...], preferred_element_type=F32)
    slot = jnp.sum(jnp.where(in_bin, rank, 0.0), axis=0, keepdims=True)
    home_row = jnp.sum(jnp.where(in_bin, home, 0.0), axis=0, keepdims=True)
    address = (home_row * LANES + slot).astype(jnp.int32)
    addr_ref[...] = jnp.broadcast_to(address, addr_ref.shape)
    label_rows = jnp.broadcast_to((ids + 1).astype(F32), (8, rows)).astype(BF16)

    fetch.wait()
    values = emb[...].astype(F32)
    scale = lax.rsqrt(jnp.mean(values * values, axis=1, keepdims=True) + EPSILON)
    unit = (values * (scale * width ** (-0.5))).astype(BF16)

    def hot(place):
        first = facing(place) * LANES
        return iota((LANES, rows), 0) + first == addr_ref[0:1, :]

    def sized(where, act):
        for size in sorted(set(caps)):
            match = functools.reduce(
                jnp.logical_or, [where == chips[r] for r in range(bins) if caps[r] == size])
            pl.when(match)(functools.partial(act, size))

    def data_copy(place, size):
        return pltpu.make_async_remote_copy(
            packed.at[place, pl.ds(0, size)], own.at[place, pl.ds(0, size)],
            send.at[place], recv.at[place], device_id={"blk": peer(place)}, device_id_type=MESH)

    def label_copy(place):
        return pltpu.make_async_remote_copy(
            packed_lab.at[place], own_lab.at[place], send_lab.at[place], recv_lab.at[place],
            device_id={"blk": peer(place)}, device_id_type=MESH)

    def forward_copy(place, size):
        return pltpu.make_async_remote_copy(
            own.at[place, pl.ds(0, size)], other.at[place, pl.ds(0, size)],
            fsend.at[place], frecv.at[place], device_id={"blk": partner}, device_id_type=MESH)

    def forward_label_copy(place):
        return pltpu.make_async_remote_copy(
            own_lab.at[place], other_lab.at[place], fsend_lab.at[place], frecv_lab.at[place],
            device_id={"blk": partner}, device_id_type=MESH)

    def return_copy(place):
        return pltpu.make_async_remote_copy(
            ret.at[place], ret_in.at[place], rsend.at[place], rrecv.at[place],
            device_id={"blk": peer(place)}, device_id_type=MESH)

    def pack(place, rows_ref, lab_ref):
        one_hot = jnp.where(hot(place), 1.0, 0.0).astype(BF16)
        rows_ref[place] = jnp.dot(one_hot, unit, preferred_element_type=F32).astype(BF16)
        lab_ref[place] = lax.dot_general(label_rows, one_hot, NT, preferred_element_type=F32)

    pack(1, packed, packed_lab)
    pl.semaphore_wait(barrier, bins)

    def send_step(s):
        if not (isinstance(s, int) and s == 0):
            pack(s + 1, packed, packed_lab)
        label_copy(s + 1).start()
        sized(facing(s + 1), lambda size: data_copy(s + 1, size).start())

    loop(bins - 1, send_step)
    pack(0, own, own_lab)
    forward_label_copy(0).start()
    sized(chip, lambda size: forward_copy(0, size).start())

    def clear(size):
        def step(s):
            if size < LANES:
                own[s + 1, size:, :] = jnp.zeros((LANES - size, width), BF16)
            if size < cap:
                other[s, size:cap, :] = jnp.zeros((cap - size, width), BF16)
        loop(bins - 1, step)
        if size < cap:
            other[bins - 1, size:cap, :] = jnp.zeros((cap - size, width), BF16)

    sized(chip, clear)

    def clear_sums(pair):
        acc_dens[pair] = jnp.zeros((8, 2 * LANES), F32)
        acc_cent[pair] = jnp.zeros((8, 2 * LANES), F32)

    loop(bins // 2, clear_sums)

    def take(place):
        label_copy(place).wait_recv()
        forward_label_copy(place).start()

        def go(size):
            data_copy(place, size).wait_recv()
            forward_copy(place, size).start()

        sized(chip, go)

    def arrived(place):
        forward_label_copy(place).wait_recv()
        sized(chip, lambda size: forward_copy(place, size).wait_recv())

    def tile(side, lab, left, count, pair, half=None):
        blocks = (0, 1) if half is None else (half,)
        part = slice(blocks[0] * LANES, (blocks[-1] + 1) * LANES)
        left_rows = side[pl.ds(left, count), :cap, :].reshape(count * cap, width)
        left_lab = jnp.concatenate([lab[left + k].T[:cap, 0:1] for k in range(count)], axis=0)
        right_rows = own[pl.ds(2 * pair + blocks[0], len(blocks))].reshape(-1, width)
        right_lab = jnp.concatenate([own_lab[2 * pair + k, 0:1, :] for k in blocks], axis=1)
        cosine = lax.dot_general(left_rows, right_rows, NT, preferred_element_type=F32)
        same = left_lab == right_lab
        dens = jnp.where(same, jnp.exp(cosine * (1.0 / SOFTMAX_TEMP)), 0.0)
        cent = jnp.where(same, cosine, 0.0)
        acc_dens[pair, :, part] += jnp.sum(dens.reshape(count * cap // 8, 8, -1), axis=0)
        acc_cent[pair, :, part] += jnp.sum(cent.reshape(count * cap // 8, 8, -1), axis=0)

    def close(pair):
        dens = jnp.sum(acc_dens[pair], axis=0, keepdims=True)
        cent = jnp.sum(acc_cent[pair], axis=0, keepdims=True)
        for half in range(2):
            part = slice(half * LANES, (half + 1) * LANES)
            ret[2 * pair + half] = jnp.concatenate(
                [dens[:, part], cent[:, part], jnp.zeros((6, LANES), F32)], axis=0)

    def span(count, body):
        if isinstance(count, int):
            loop(count, body)
        else:
            lax.fori_loop(0, count, lambda step, carry: (body(step), carry)[1], 0)

    def group(pair):
        span(pair, lambda q: tile(own, own_lab, 2 * pair, 2, q))
        span(pair, lambda q: tile(own, own_lab, 2 * q, 2, pair))
        tile(own, own_lab, 2 * pair, 2, pair)
        span(pair, lambda q: tile(other, other_lab, 2 * q, 2, pair))
        arrived(2 * pair)
        arrived(2 * pair + 1)
        span(pair, lambda q: tile(other, other_lab, 2 * pair, 2, q))
        tile(other, other_lab, 2 * pair, 2, pair)

    pairs = bins // 2
    take(1)
    group(0)

    def middle(s):
        take(2 * s + 2)
        take(2 * s + 3)
        group(s + 1)

    loop(pairs - 2, middle)
    last = pairs - 1
    next_last, very_last = 2 * last, 2 * last + 1
    take(next_last)
    span(last, lambda q: tile(own, own_lab, next_last, 1, q))
    span(last, lambda q: tile(own, own_lab, 2 * q, 2, last, 0))
    tile(own, own_lab, next_last, 1, last, 0)
    span(last, lambda q: tile(other, other_lab, 2 * q, 2, last, 0))
    arrived(next_last)
    span(last, lambda q: tile(other, other_lab, next_last, 1, q))
    tile(other, other_lab, next_last, 1, last, 0)
    take(very_last)
    span(last, lambda q: tile(own, own_lab, very_last, 1, q))
    tile(own, own_lab, very_last, 1, last, 0)
    span(pairs, lambda q: tile(own, own_lab, 2 * q, 2, last, 1))
    span(last, lambda q: tile(other, other_lab, 2 * q, 2, last, 1))
    tile(other, other_lab, next_last, 1, last, 1)
    arrived(very_last)
    tile(other, other_lab, very_last, 1, 0)
    close(0)
    ret_in[0] = ret[0]
    return_copy(1).start()

    def answer(s):
        tile(other, other_lab, very_last, 1, s + 1)
        close(s + 1)
        return_copy(2 * s + 2).start()
        return_copy(2 * s + 3).start()

    loop(pairs - 1, answer)

    def finish(s):
        sized(facing(s + 1), lambda size: data_copy(s + 1, size).wait_send())
        label_copy(s + 1).wait_send()

    loop(bins - 1, finish)

    def finish_forward(s):
        sized(chip, lambda size: forward_copy(s, size).wait_send())
        forward_label_copy(s).wait_send()

    loop(bins, finish_forward)

    def gathered(place, total):
        values = ret_in[place].T
        mine = hot(place)
        return (total[0] + jnp.where(mine, values[:, 0:1], 0.0),
                total[1] + jnp.where(mine, values[:, 1:2], 0.0))

    none = jnp.zeros((LANES, rows), F32)
    total = gathered(0, (none, none))

    def collect(place, total):
        return_copy(place).wait_recv()
        return gathered(place, total)

    if bins <= 8:
        for place in range(1, bins):
            total = collect(place, total)
    else:
        total = lax.fori_loop(1, bins, collect, total)
    dens = jnp.sum(total[0], axis=0, keepdims=True) / size_row
    cent = jnp.sum(total[1], axis=0, keepdims=True) / size_row
    out_ref[...] = jnp.concatenate([jnp.log(dens), cent, jnp.zeros((6, rows), F32)], axis=0)

    loop(bins - 1, lambda s: return_copy(s + 1).wait_send())


def on_device(embeddings, cluster_ids, cluster_sizes):
    n = lax.axis_size("blk")
    rows, width = embeddings.shape
    bins = n // 2
    total = rows * n
    limit = max(2 * total // bins, total * 5 // 32)
    caps = [-(-min(-(-limit // n), -(-rows // (r + 1))) // 16) * 16 for r in range(bins)]
    cap = caps[0]
    chips = []
    for r in range(bins // 2):
        low, high = bins // 2 - 1 - r, bins // 2 + r
        chips += [low, high] if r % 2 == 0 else [high, low]
    vmem = pl.BlockSpec(memory_space=pltpu.VMEM)
    hbm = pl.BlockSpec(memory_space=pltpu.HBM)
    dma = pltpu.SemaphoreType.DMA((bins,))
    out = pl.pallas_call(
        functools.partial(kernel, n, cap, tuple(caps), tuple(chips), float(limit)),
        out_shape=jax.ShapeDtypeStruct((8, rows), F32),
        in_specs=[hbm] * 3,
        out_specs=vmem,
        scratch_shapes=[
            pltpu.VMEM((rows, width), BF16),
            pltpu.VMEM(cluster_ids.shape, jnp.int32),
            pltpu.VMEM(cluster_sizes.shape, jnp.int32),
            pltpu.VMEM((bins, LANES, width), BF16),
            pltpu.VMEM((bins, 8, LANES), F32),
            pltpu.VMEM((bins, LANES, width), BF16),
            pltpu.VMEM((bins, LANES, width), BF16),
            pltpu.VMEM((bins, 8, LANES), F32),
            pltpu.VMEM((bins, 8, LANES), F32),
            pltpu.VMEM((bins, 8, LANES), F32),
            pltpu.VMEM((bins, 8, LANES), F32),
            pltpu.VMEM((8, rows), jnp.int32),
            pltpu.VMEM((bins // 2, 8, 2 * LANES), F32),
            pltpu.VMEM((bins // 2, 8, 2 * LANES), F32),
            pltpu.VMEM((rows, rows), BF16),
            pltpu.SemaphoreType.DMA,
            pltpu.SemaphoreType.DMA,
            pltpu.SemaphoreType.DMA,
        ] + [dma] * 10,
        compiler_params=pltpu.CompilerParams(
            collective_id=0, has_side_effects=True, vmem_limit_bytes=64 * 1024 * 1024 - 128 * 1024),
        cost_estimate=pl.CostEstimate(flops=4 * 10 ** 9, bytes_accessed=10 ** 6, transcendentals=0),
    )(embeddings, cluster_ids, cluster_sizes)
    return out[0], out[1]


def solution(mesh):
    in_specs = (P(("groups", "blk"), None), P(("groups", "blk")), P("groups"))
    out_specs = (P(("groups", "blk")), P(("groups", "blk")))
    return jax.shard_map(
        on_device, mesh=mesh, in_specs=in_specs, out_specs=out_specs, check_vma=False
    )
```

```python
import functools

import jax
import jax.numpy as jnp
from jax import lax
from jax.experimental import pallas as pl
from jax.experimental.pallas import tpu as pltpu
from jax.sharding import PartitionSpec as P

SOFTMAX_TEMP = 0.1
EPSILON = 1e-06
LANES = 128
IN_FLIGHT = 3
MESH = pl.DeviceIdType.MESH
F32 = jnp.float32
BF16 = jnp.bfloat16
NT = (((1,), (1,)), ((), ()))


def iota(shape, dim):
    return lax.broadcasted_iota(jnp.int32, shape, dim)


def loop(count, body):
    if count <= 8:
        for step in range(count):
            body(step)
    else:
        lax.fori_loop(0, count, lambda step, carry: (body(step), carry)[1], 0)


def kernel(n, cap, caps, chips, limit, emb_hbm, ids_hbm, sizes_hbm, out_ref,
           emb, ids_ref, sizes_ref, packed, packed_lab, own, other, own_lab, other_lab, ret, ret_in, addr_ref,
           acc_dens, acc_cent, emb_sem, ids_sem, sizes_sem,
           send, recv, send_lab, recv_lab, fsend, frecv, fsend_lab, frecv_lab, rsend, rrecv):
    bins = n // 2
    rows, width = emb.shape
    clusters = sizes_ref.shape[0]
    me = lax.axis_index("blk")
    chip = lax.div(me, 2)
    core = lax.rem(me, 2)
    partner = 2 * chip + 1 - core

    def turn(place):
        if isinstance(place, int) and place == 0:
            return jnp.int32(0)
        place = jnp.int32(place)
        half = lax.div(place, 2)
        odd = lax.rem(place, 2)
        first = odd * (bins // 2 + half) + (1 - odd) * half
        second = odd * (half + 1) + (1 - odd) * (bins // 2 + half - 1)
        at_end = lax.div(place, bins - 1)
        second = at_end * (bins - 1) + (1 - at_end) * second
        return first + core * (second - first)

    def facing(place):
        change, other_chip, bit = turn(place), chip, 1
        while bit < bins:
            flip = lax.rem(lax.div(change, bit), 2)
            other_chip = other_chip + flip * bit * (1 - 2 * lax.rem(lax.div(chip, bit), 2))
            bit *= 2
        return other_chip

    def peer(place):
        return 2 * facing(place) + core

    fetch = pltpu.make_async_copy(emb_hbm, emb, emb_sem)
    fetch_ids = pltpu.make_async_copy(ids_hbm, ids_ref, ids_sem)
    fetch_sizes = pltpu.make_async_copy(sizes_hbm, sizes_ref, sizes_sem)
    fetch_sizes.start()
    fetch_ids.start()
    fetch.start()
    barrier = pltpu.get_barrier_semaphore()
    pl.semaphore_signal(barrier, inc=1, device_id={"blk": partner}, device_id_type=MESH)
    loop(bins - 1, lambda s: pl.semaphore_signal(
        barrier, inc=1, device_id={"blk": peer(s + 1)}, device_id_type=MESH))

    fetch_sizes.wait()
    sizes_row = sizes_ref[...].reshape(1, clusters).astype(F32)
    above = iota((clusters, clusters), 0)
    along = iota((clusters, clusters), 1)
    ends = jnp.sum(jnp.where(along <= above, sizes_row, 0.0), axis=1, keepdims=True)
    sizes = jnp.sum(jnp.where(along == above, sizes_row, 0.0), axis=1, keepdims=True)
    starts = ends - sizes
    shown = max(bins, 8)
    edge = jnp.zeros((1, 1), F32)
    bin_of = jnp.zeros((clusters, 1), F32)
    load = jnp.zeros((shown, 1), F32)
    load_row = jnp.zeros((1, LANES), F32)
    for index in range(bins):
        filled = edge
        edge = jnp.max(jnp.where(ends <= edge + limit, ends, 0.0), axis=0, keepdims=True)
        bin_of += jnp.where(starts >= edge, 1.0, 0.0)
        load = jnp.where(iota((shown, 1), 0) == index, edge - filled, load)
        load_row = jnp.where(iota((1, LANES), 1) == index, edge - filled, load_row)
    earlier = iota((shown, LANES), 1) < iota((shown, LANES), 0)
    ahead = (load_row > load) | ((load_row == load) & earlier)
    ahead = ahead & (iota((shown, LANES), 1) < bins)
    order = jnp.sum(jnp.where(ahead, 1.0, 0.0), axis=1, keepdims=True)
    home = jnp.zeros((shown, 1), F32)
    for place in range(bins):
        home = jnp.where(order == place, float(chips[place]), home)

    fetch_ids.wait()
    ids = ids_ref[...].reshape(1, rows)
    member = iota((clusters, rows), 0) == ids
    bin_row = jnp.sum(jnp.where(member, bin_of, 0.0), axis=0, keepdims=True)
    size_row = jnp.sum(jnp.where(member, sizes, 0.0), axis=0, keepdims=True)
    in_bin = iota((shown, rows), 0).astype(F32) == bin_row
    before = jnp.where(iota((rows, rows), 0) < iota((rows, rows), 1), 1.0, 0.0).astype(BF16)
    rank = jnp.dot(jnp.where(in_bin, 1.0, 0.0).astype(BF16), before, preferred_element_type=F32)
    slot = jnp.sum(jnp.where(in_bin, rank, 0.0), axis=0, keepdims=True)
    home_row = jnp.sum(jnp.where(in_bin, home, 0.0), axis=0, keepdims=True)
    address = (home_row * LANES + slot).astype(jnp.int32)
    addr_ref[...] = jnp.broadcast_to(address, addr_ref.shape)
    label_rows = jnp.broadcast_to((ids + 1).astype(F32), (8, rows)).astype(BF16)

    fetch.wait()
    values = emb[...].astype(F32)
    scale = lax.rsqrt(jnp.mean(values * values, axis=1, keepdims=True) + EPSILON)
    unit = (values * (scale * width ** (-0.5))).astype(BF16)

    def hot(place):
        first = facing(place) * LANES
        return iota((LANES, rows), 0) + first == addr_ref[0:1, :]

    def sized(where, act):
        for size in sorted(set(caps)):
            match = functools.reduce(
                jnp.logical_or, [where == chips[r] for r in range(bins) if caps[r] == size])
            pl.when(match)(functools.partial(act, size))

    def data_copy(place, size):
        return pltpu.make_async_remote_copy(
            packed.at[place, pl.ds(0, size)], own.at[place, pl.ds(0, size)],
            send.at[place], recv.at[place], device_id={"blk": peer(place)}, device_id_type=MESH)

    def label_copy(place):
        return pltpu.make_async_remote_copy(
            packed_lab.at[place], own_lab.at[place], send_lab.at[place], recv_lab.at[place],
            device_id={"blk": peer(place)}, device_id_type=MESH)

    def forward_copy(place, size):
        return pltpu.make_async_remote_copy(
            own.at[place, pl.ds(0, size)], other.at[place, pl.ds(0, size)],
            fsend.at[place], frecv.at[place], device_id={"blk": partner}, device_id_type=MESH)

    def forward_label_copy(place):
        return pltpu.make_async_remote_copy(
            own_lab.at[place], other_lab.at[place], fsend_lab.at[place], frecv_lab.at[place],
            device_id={"blk": partner}, device_id_type=MESH)

    def return_copy(place):
        return pltpu.make_async_remote_copy(
            ret.at[place], ret_in.at[place], rsend.at[place], rrecv.at[place],
            device_id={"blk": peer(place)}, device_id_type=MESH)

    def pack(place, rows_ref, lab_ref):
        one_hot = jnp.where(hot(place), 1.0, 0.0).astype(BF16)
        rows_ref[place] = jnp.dot(one_hot, unit, preferred_element_type=F32).astype(BF16)
        lab_ref[place] = lax.dot_general(label_rows, one_hot, NT, preferred_element_type=F32)

    pl.semaphore_wait(barrier, bins)

    def start_send(place):
        label_copy(place).start()
        sized(facing(place), lambda size: data_copy(place, size).start())

    ahead_by = min(IN_FLIGHT, bins - 1)
    for place in range(1, ahead_by + 1):
        pack(place, packed, packed_lab)
        start_send(place)
    pack(0, own, own_lab)
    forward_label_copy(0).start()
    sized(chip, lambda size: forward_copy(0, size).start())
    loop(bins - 1 - ahead_by, lambda s: pack(s + 1 + ahead_by, packed, packed_lab))

    def clear(size):
        def step(s):
            if size < LANES:
                own[s + 1, size:, :] = jnp.zeros((LANES - size, width), BF16)
            if size < cap:
                other[s, size:cap, :] = jnp.zeros((cap - size, width), BF16)
        loop(bins - 1, step)
        if size < cap:
            other[bins - 1, size:cap, :] = jnp.zeros((cap - size, width), BF16)

    sized(chip, clear)

    def clear_sums(pair):
        acc_dens[pair] = jnp.zeros((8, 2 * LANES), F32)
        acc_cent[pair] = jnp.zeros((8, 2 * LANES), F32)

    loop(bins // 2, clear_sums)

    def take(place):
        label_copy(place).wait_recv()
        forward_label_copy(place).start()

        def go(size):
            data_copy(place, size).wait_recv()
            forward_copy(place, size).start()

        sized(chip, go)
        if not isinstance(place, int):
            pl.when(place + ahead_by < bins)(lambda: start_send(place + ahead_by))
        elif place + ahead_by < bins:
            start_send(place + ahead_by)

    def arrived(place):
        forward_label_copy(place).wait_recv()
        sized(chip, lambda size: forward_copy(place, size).wait_recv())

    def tile(side, lab, left, right):
        left_rows = side[pl.ds(2 * left, 2), :cap, :].reshape(2 * cap, width)
        left_lab = jnp.concatenate(
            [lab[2 * left + half].T[:cap, 0:1] for half in range(2)], axis=0)
        right_rows = own[pl.ds(2 * right, 2)].reshape(2 * LANES, width)
        right_lab = jnp.concatenate(
            [own_lab[2 * right + half, 0:1, :] for half in range(2)], axis=1)
        cosine = lax.dot_general(left_rows, right_rows, NT, preferred_element_type=F32)
        same = left_lab == right_lab
        dens = jnp.where(same, jnp.exp(cosine * (1.0 / SOFTMAX_TEMP)), 0.0)
        cent = jnp.where(same, cosine, 0.0)
        acc_dens[right] += jnp.sum(dens.reshape(2 * cap // 8, 8, 2 * LANES), axis=0)
        acc_cent[right] += jnp.sum(cent.reshape(2 * cap // 8, 8, 2 * LANES), axis=0)

    def close(pair):
        dens = jnp.sum(acc_dens[pair], axis=0, keepdims=True)
        cent = jnp.sum(acc_cent[pair], axis=0, keepdims=True)
        for half in range(2):
            part = slice(half * LANES, (half + 1) * LANES)
            ret[2 * pair + half] = jnp.concatenate(
                [dens[:, part], cent[:, part], jnp.zeros((6, LANES), F32)], axis=0)

    def span(count, body):
        if isinstance(count, int):
            loop(count, body)
        else:
            lax.fori_loop(0, count, lambda step, carry: (body(step), carry)[1], 0)

    def group(pair):
        span(pair, lambda q: tile(own, own_lab, pair, q))
        span(pair, lambda q: tile(own, own_lab, q, pair))
        tile(own, own_lab, pair, pair)
        span(pair, lambda q: tile(other, other_lab, q, pair))
        arrived(2 * pair)
        arrived(2 * pair + 1)

    def finish_group(pair):
        span(pair, lambda q: tile(other, other_lab, pair, q))
        tile(other, other_lab, pair, pair)

    pairs = bins // 2
    take(1)
    group(0)
    finish_group(0)

    def middle(s):
        take(2 * s + 2)
        take(2 * s + 3)
        group(s + 1)
        finish_group(s + 1)

    loop(pairs - 2, middle)
    last = pairs - 1
    take(2 * last)
    take(2 * last + 1)
    group(last)
    tile(other, other_lab, last, 0)
    close(0)
    ret_in[0] = ret[0]
    return_copy(1).start()

    def answer(s):
        tile(other, other_lab, last, s + 1)
        close(s + 1)
        return_copy(2 * s + 2).start()
        return_copy(2 * s + 3).start()

    loop(pairs - 1, answer)

    def gathered(place, total):
        values = ret_in[place].T
        mine = hot(place)
        return (total[0] + jnp.where(mine, values[:, 0:1], 0.0),
                total[1] + jnp.where(mine, values[:, 1:2], 0.0))

    none = jnp.zeros((LANES, rows), F32)
    total = gathered(0, (none, none))

    def collect(place, total):
        return_copy(place).wait_recv()
        return gathered(place, total)

    if bins <= 8:
        for place in range(1, bins):
            total = collect(place, total)
    else:
        total = lax.fori_loop(1, bins, collect, total)
    dens = jnp.sum(total[0], axis=0, keepdims=True) / size_row
    cent = jnp.sum(total[1], axis=0, keepdims=True) / size_row
    out_ref[...] = jnp.concatenate([jnp.log(dens), cent, jnp.zeros((6, rows), F32)], axis=0)

    def finish(s):
        sized(facing(s + 1), lambda size: data_copy(s + 1, size).wait_send())
        label_copy(s + 1).wait_send()
        return_copy(s + 1).wait_send()

    loop(bins - 1, finish)

    def finish_forward(s):
        sized(chip, lambda size: forward_copy(s, size).wait_send())
        forward_label_copy(s).wait_send()

    loop(bins, finish_forward)


def on_device(embeddings, cluster_ids, cluster_sizes):
    n = lax.axis_size("blk")
    rows, width = embeddings.shape
    bins = n // 2
    total = rows * n
    limit = max(2 * total // bins, total * 5 // 32)
    caps = [-(-min(-(-limit // n), -(-rows // (r + 1))) // 16) * 16 for r in range(bins)]
    cap = caps[0]
    chips = []
    for r in range(bins // 2):
        low, high = bins // 2 - 1 - r, bins // 2 + r
        chips += [low, high] if r % 2 == 0 else [high, low]
    vmem = pl.BlockSpec(memory_space=pltpu.VMEM)
    hbm = pl.BlockSpec(memory_space=pltpu.HBM)
    dma = pltpu.SemaphoreType.DMA((bins,))
    out = pl.pallas_call(
        functools.partial(kernel, n, cap, tuple(caps), tuple(chips), float(limit)),
        out_shape=jax.ShapeDtypeStruct((8, rows), F32),
        in_specs=[hbm] * 3,
        out_specs=vmem,
        scratch_shapes=[
            pltpu.VMEM((rows, width), BF16),
            pltpu.VMEM(cluster_ids.shape, jnp.int32),
            pltpu.VMEM(cluster_sizes.shape, jnp.int32),
            pltpu.VMEM((bins, LANES, width), BF16),
            pltpu.VMEM((bins, 8, LANES), F32),
            pltpu.VMEM((bins, LANES, width), BF16),
            pltpu.VMEM((bins, LANES, width), BF16),
            pltpu.VMEM((bins, 8, LANES), F32),
            pltpu.VMEM((bins, 8, LANES), F32),
            pltpu.VMEM((bins, 8, LANES), F32),
            pltpu.VMEM((bins, 8, LANES), F32),
            pltpu.VMEM((8, rows), jnp.int32),
            pltpu.VMEM((bins // 2, 8, 2 * LANES), F32),
            pltpu.VMEM((bins // 2, 8, 2 * LANES), F32),
            pltpu.SemaphoreType.DMA,
            pltpu.SemaphoreType.DMA,
            pltpu.SemaphoreType.DMA,
        ] + [dma] * 10,
        compiler_params=pltpu.CompilerParams(
            collective_id=0, has_side_effects=True, vmem_limit_bytes=48 * 1024 * 1024),
        cost_estimate=pl.CostEstimate(flops=4 * 10 ** 9, bytes_accessed=10 ** 6, transcendentals=0),
    )(*[pltpu.with_memory_space_constraint(x, pltpu.HBM) for x in (embeddings, cluster_ids, cluster_sizes)])
    return out[0], out[1]


def solution(mesh):
    in_specs = (P(("groups", "blk"), None), P(("groups", "blk")), P("groups"))
    out_specs = (P(("groups", "blk")), P(("groups", "blk")))
    return jax.shard_map(
        on_device, mesh=mesh, in_specs=in_specs, out_specs=out_specs, check_vma=False
    )
```

```python
import functools

import jax
import jax.numpy as jnp
from jax import lax
from jax.experimental import pallas as pl
from jax.experimental.pallas import tpu as pltpu
from jax.sharding import PartitionSpec as P

SOFTMAX_TEMP = 0.1
EPSILON = 1e-06
LANES = 128
MESH = pl.DeviceIdType.MESH
F32 = jnp.float32
BF16 = jnp.bfloat16
NT = (((1,), (1,)), ((), ()))


def iota(shape, dim):
    return lax.broadcasted_iota(jnp.int32, shape, dim)


def loop(count, body):
    if count <= 8:
        for step in range(count):
            body(step)
    else:
        lax.fori_loop(0, count, lambda step, carry: (body(step), carry)[1], 0)


def kernel(n, cap, caps, chips, limit, emb_hbm, ids_hbm, sizes_hbm, out_ref,
           emb, ids_ref, sizes_ref, packed, packed_lab, own, other, own_lab, other_lab, ret, ret_in, addr_ref,
           acc_dens, acc_cent, emb_sem, ids_sem, sizes_sem,
           send, recv, send_lab, recv_lab, fsend, frecv, fsend_lab, frecv_lab, rsend, rrecv):
    bins = n // 2
    rows, width = emb.shape
    clusters = sizes_ref.shape[0]
    me = lax.axis_index("blk")
    chip = lax.div(me, 2)
    core = lax.rem(me, 2)
    partner = 2 * chip + 1 - core

    def turn(place):
        if isinstance(place, int) and place == 0:
            return jnp.int32(0)
        place = jnp.int32(place)
        half = lax.div(place, 2)
        odd = lax.rem(place, 2)
        first = odd * (bins // 2 + half) + (1 - odd) * half
        second = odd * (half + 1) + (1 - odd) * (bins // 2 + half - 1)
        at_end = lax.div(place, bins - 1)
        second = at_end * (bins - 1) + (1 - at_end) * second
        return first + core * (second - first)

    def facing(place):
        change, other_chip, bit = turn(place), chip, 1
        while bit < bins:
            flip = lax.rem(lax.div(change, bit), 2)
            other_chip = other_chip + flip * bit * (1 - 2 * lax.rem(lax.div(chip, bit), 2))
            bit *= 2
        return other_chip

    def peer(place):
        return 2 * facing(place) + core

    fetch = pltpu.make_async_copy(emb_hbm, emb, emb_sem)
    fetch_ids = pltpu.make_async_copy(ids_hbm, ids_ref, ids_sem)
    fetch_sizes = pltpu.make_async_copy(sizes_hbm, sizes_ref, sizes_sem)
    fetch_sizes.start()
    fetch_ids.start()
    fetch.start()
    barrier = pltpu.get_barrier_semaphore()
    pl.semaphore_signal(barrier, inc=1, device_id={"blk": partner}, device_id_type=MESH)
    loop(bins - 1, lambda s: pl.semaphore_signal(
        barrier, inc=1, device_id={"blk": peer(s + 1)}, device_id_type=MESH))

    fetch_sizes.wait()
    sizes_row = sizes_ref[...].reshape(1, clusters).astype(F32)
    above = iota((clusters, clusters), 0)
    along = iota((clusters, clusters), 1)
    ends = jnp.sum(jnp.where(along <= above, sizes_row, 0.0), axis=1, keepdims=True)
    sizes = jnp.sum(jnp.where(along == above, sizes_row, 0.0), axis=1, keepdims=True)
    starts = ends - sizes
    shown = max(bins, 8)
    edge = jnp.zeros((1, 1), F32)
    bin_of = jnp.zeros((clusters, 1), F32)
    load = jnp.zeros((shown, 1), F32)
    load_row = jnp.zeros((1, LANES), F32)
    for index in range(bins):
        filled = edge
        edge = jnp.max(jnp.where(ends <= edge + limit, ends, 0.0), axis=0, keepdims=True)
        bin_of += jnp.where(starts >= edge, 1.0, 0.0)
        load = jnp.where(iota((shown, 1), 0) == index, edge - filled, load)
        load_row = jnp.where(iota((1, LANES), 1) == index, edge - filled, load_row)
    earlier = iota((shown, LANES), 1) < iota((shown, LANES), 0)
    ahead = (load_row > load) | ((load_row == load) & earlier)
    ahead = ahead & (iota((shown, LANES), 1) < bins)
    order = jnp.sum(jnp.where(ahead, 1.0, 0.0), axis=1, keepdims=True)
    home = jnp.zeros((shown, 1), F32)
    for place in range(bins):
        home = jnp.where(order == place, float(chips[place]), home)

    fetch_ids.wait()
    ids = ids_ref[...].reshape(1, rows)
    member = iota((clusters, rows), 0) == ids
    bin_row = jnp.sum(jnp.where(member, bin_of, 0.0), axis=0, keepdims=True)
    size_row = jnp.sum(jnp.where(member, sizes, 0.0), axis=0, keepdims=True)
    in_bin = iota((shown, rows), 0).astype(F32) == bin_row
    before = jnp.where(iota((rows, rows), 0) < iota((rows, rows), 1), 1.0, 0.0).astype(BF16)
    rank = jnp.dot(jnp.where(in_bin, 1.0, 0.0).astype(BF16), before, preferred_element_type=F32)
    slot = jnp.sum(jnp.where(in_bin, rank, 0.0), axis=0, keepdims=True)
    home_row = jnp.sum(jnp.where(in_bin, home, 0.0), axis=0, keepdims=True)
    address = (home_row * LANES + slot).astype(jnp.int32)
    addr_ref[...] = jnp.broadcast_to(address, addr_ref.shape)
    label_rows = jnp.broadcast_to((ids + 1).astype(F32), (8, rows)).astype(BF16)

    fetch.wait()
    values = emb[...].astype(F32)
    scale = lax.rsqrt(jnp.mean(values * values, axis=1, keepdims=True) + EPSILON)
    unit = (values * (scale * width ** (-0.5))).astype(BF16)

    def hot(place):
        first = facing(place) * LANES
        return iota((LANES, rows), 0) + first == addr_ref[0:1, :]

    def sized(where, act):
        for size in sorted(set(caps)):
            match = functools.reduce(
                jnp.logical_or, [where == chips[r] for r in range(bins) if caps[r] == size])
            pl.when(match)(functools.partial(act, size))

    def data_copy(place, size):
        return pltpu.make_async_remote_copy(
            packed.at[place, pl.ds(0, size)], own.at[place, pl.ds(0, size)],
            send.at[place], recv.at[place], device_id={"blk": peer(place)}, device_id_type=MESH)

    def label_copy(place):
        return pltpu.make_async_remote_copy(
            packed_lab.at[place], own_lab.at[place], send_lab.at[place], recv_lab.at[place],
            device_id={"blk": peer(place)}, device_id_type=MESH)

    def forward_copy(place, size):
        return pltpu.make_async_remote_copy(
            own.at[place, pl.ds(0, size)], other.at[place, pl.ds(0, size)],
            fsend.at[place], frecv.at[place], device_id={"blk": partner}, device_id_type=MESH)

    def forward_label_copy(place):
        return pltpu.make_async_remote_copy(
            own_lab.at[place], other_lab.at[place], fsend_lab.at[place], frecv_lab.at[place],
            device_id={"blk": partner}, device_id_type=MESH)

    def return_copy(place):
        return pltpu.make_async_remote_copy(
            ret.at[place], ret_in.at[place], rsend.at[place], rrecv.at[place],
            device_id={"blk": peer(place)}, device_id_type=MESH)

    def pack(place, rows_ref, lab_ref):
        one_hot = jnp.where(hot(place), 1.0, 0.0).astype(BF16)
        rows_ref[place] = jnp.dot(one_hot, unit, preferred_element_type=F32).astype(BF16)
        lab_ref[place] = lax.dot_general(label_rows, one_hot, NT, preferred_element_type=F32)

    pl.semaphore_wait(barrier, bins)

    def send_step(s):
        pack(s + 1, packed, packed_lab)
        label_copy(s + 1).start()
        sized(facing(s + 1), lambda size: data_copy(s + 1, size).start())

    loop(bins - 1, send_step)
    pack(0, own, own_lab)
    forward_label_copy(0).start()
    sized(chip, lambda size: forward_copy(0, size).start())

    def clear(size):
        def step(s):
            if size < LANES:
                own[s + 1, size:, :] = jnp.zeros((LANES - size, width), BF16)
            if size < cap:
                other[s, size:cap, :] = jnp.zeros((cap - size, width), BF16)
        loop(bins - 1, step)
        if size < cap:
            other[bins - 1, size:cap, :] = jnp.zeros((cap - size, width), BF16)

    sized(chip, clear)

    def clear_sums(pair):
        acc_dens[pair] = jnp.zeros((8, 2 * LANES), F32)
        acc_cent[pair] = jnp.zeros((8, 2 * LANES), F32)

    loop(bins // 2, clear_sums)

    def take(place):
        label_copy(place).wait_recv()
        forward_label_copy(place).start()

        def go(size):
            data_copy(place, size).wait_recv()
            forward_copy(place, size).start()

        sized(chip, go)

    def arrived(place):
        forward_label_copy(place).wait_recv()
        sized(chip, lambda size: forward_copy(place, size).wait_recv())

    def tile(side, lab, left, right):
        left_rows = side[pl.ds(2 * left, 2), :cap, :].reshape(2 * cap, width)
        left_lab = jnp.concatenate(
            [lab[2 * left + half].T[:cap, 0:1] for half in range(2)], axis=0)
        right_rows = own[pl.ds(2 * right, 2)].reshape(2 * LANES, width)
        right_lab = jnp.concatenate(
            [own_lab[2 * right + half, 0:1, :] for half in range(2)], axis=1)
        cosine = lax.dot_general(left_rows, right_rows, NT, preferred_element_type=F32)
        same = left_lab == right_lab
        dens = jnp.where(same, jnp.exp(cosine * (1.0 / SOFTMAX_TEMP)), 0.0)
        cent = jnp.where(same, cosine, 0.0)
        acc_dens[right] += jnp.sum(dens.reshape(2 * cap // 8, 8, 2 * LANES), axis=0)
        acc_cent[right] += jnp.sum(cent.reshape(2 * cap // 8, 8, 2 * LANES), axis=0)

    def close(pair):
        dens = jnp.sum(acc_dens[pair], axis=0, keepdims=True)
        cent = jnp.sum(acc_cent[pair], axis=0, keepdims=True)
        for half in range(2):
            part = slice(half * LANES, (half + 1) * LANES)
            ret[2 * pair + half] = jnp.concatenate(
                [dens[:, part], cent[:, part], jnp.zeros((6, LANES), F32)], axis=0)

    def span(count, body):
        if isinstance(count, int):
            loop(count, body)
        else:
            lax.fori_loop(0, count, lambda step, carry: (body(step), carry)[1], 0)

    def group(pair):
        span(pair, lambda q: tile(own, own_lab, pair, q))
        span(pair, lambda q: tile(own, own_lab, q, pair))
        tile(own, own_lab, pair, pair)
        span(pair, lambda q: tile(other, other_lab, q, pair))
        arrived(2 * pair)
        arrived(2 * pair + 1)

    def finish_group(pair):
        span(pair, lambda q: tile(other, other_lab, pair, q))
        tile(other, other_lab, pair, pair)

    pairs = bins // 2
    take(1)
    group(0)
    finish_group(0)

    def middle(s):
        take(2 * s + 2)
        take(2 * s + 3)
        group(s + 1)
        finish_group(s + 1)

    loop(pairs - 2, middle)
    last = pairs - 1
    take(2 * last)
    take(2 * last + 1)
    group(last)
    tile(other, other_lab, last, 0)
    close(0)
    ret_in[0] = ret[0]
    return_copy(1).start()

    def answer(s):
        tile(other, other_lab, last, s + 1)
        close(s + 1)
        return_copy(2 * s + 2).start()
        return_copy(2 * s + 3).start()

    loop(pairs - 1, answer)

    def gathered(place, total):
        values = ret_in[place].T
        mine = hot(place)
        return (total[0] + jnp.where(mine, values[:, 0:1], 0.0),
                total[1] + jnp.where(mine, values[:, 1:2], 0.0))

    none = jnp.zeros((LANES, rows), F32)
    total = gathered(0, (none, none))

    def collect(place, total):
        return_copy(place).wait_recv()
        return gathered(place, total)

    if bins <= 8:
        for place in range(1, bins):
            total = collect(place, total)
    else:
        total = lax.fori_loop(1, bins, collect, total)
    dens = jnp.sum(total[0], axis=0, keepdims=True) / size_row
    cent = jnp.sum(total[1], axis=0, keepdims=True) / size_row
    out_ref[...] = jnp.concatenate([jnp.log(dens), cent, jnp.zeros((6, rows), F32)], axis=0)

    def finish(s):
        sized(facing(s + 1), lambda size: data_copy(s + 1, size).wait_send())
        label_copy(s + 1).wait_send()
        return_copy(s + 1).wait_send()

    loop(bins - 1, finish)

    def finish_forward(s):
        sized(chip, lambda size: forward_copy(s, size).wait_send())
        forward_label_copy(s).wait_send()

    loop(bins, finish_forward)


def on_device(embeddings, cluster_ids, cluster_sizes):
    n = lax.axis_size("blk")
    rows, width = embeddings.shape
    bins = n // 2
    total = rows * n
    limit = max(2 * total // bins, total * 5 // 32)
    caps = [-(-min(-(-limit // n), -(-rows // (r + 1))) // 16) * 16 for r in range(bins)]
    cap = caps[0]
    chips = []
    for r in range(bins // 2):
        low, high = bins // 2 - 1 - r, bins // 2 + r
        chips += [low, high] if r % 2 == 0 else [high, low]
    vmem = pl.BlockSpec(memory_space=pltpu.VMEM)
    hbm = pl.BlockSpec(memory_space=pltpu.HBM)
    dma = pltpu.SemaphoreType.DMA((bins,))
    out = pl.pallas_call(
        functools.partial(kernel, n, cap, tuple(caps), tuple(chips), float(limit)),
        out_shape=jax.ShapeDtypeStruct((8, rows), F32),
        in_specs=[hbm] * 3,
        out_specs=vmem,
        scratch_shapes=[
            pltpu.VMEM((rows, width), BF16),
            pltpu.VMEM(cluster_ids.shape, jnp.int32),
            pltpu.VMEM(cluster_sizes.shape, jnp.int32),
            pltpu.VMEM((bins, LANES, width), BF16),
            pltpu.VMEM((bins, 8, LANES), F32),
            pltpu.VMEM((bins, LANES, width), BF16),
            pltpu.VMEM((bins, LANES, width), BF16),
            pltpu.VMEM((bins, 8, LANES), F32),
            pltpu.VMEM((bins, 8, LANES), F32),
            pltpu.VMEM((bins, 8, LANES), F32),
            pltpu.VMEM((bins, 8, LANES), F32),
            pltpu.VMEM((8, rows), jnp.int32),
            pltpu.VMEM((bins // 2, 8, 2 * LANES), F32),
            pltpu.VMEM((bins // 2, 8, 2 * LANES), F32),
            pltpu.SemaphoreType.DMA,
            pltpu.SemaphoreType.DMA,
            pltpu.SemaphoreType.DMA,
        ] + [dma] * 10,
        compiler_params=pltpu.CompilerParams(
            collective_id=0, has_side_effects=True, vmem_limit_bytes=48 * 1024 * 1024),
        cost_estimate=pl.CostEstimate(flops=4 * 10 ** 9, bytes_accessed=10 ** 6, transcendentals=0),
    )(*[pltpu.with_memory_space_constraint(x, pltpu.HBM) for x in (embeddings, cluster_ids, cluster_sizes)])
    return out[0], out[1]


def solution(mesh):
    in_specs = (P(("groups", "blk"), None), P(("groups", "blk")), P("groups"))
    out_specs = (P(("groups", "blk")), P(("groups", "blk")))
    return jax.shard_map(
        on_device, mesh=mesh, in_specs=in_specs, out_specs=out_specs, check_vma=False
    )
```
